256 devices in a mesh: group: 8 (over z_lo, core), expert: 32 (over x, y, z_hi).
Axes of the slice: x: 4, y: 4, z: 8 (z_hi: 2, z_lo: 4; z = z_hi * 4 + z_lo), core: 2. Of those that a mesh axis runs over, the one named last changes fastest.
Arguments:
- q_latent: bfloat16 [2048, 64, 512], P('group', 'expert'), may hold values from -4 to 4
- q_rope: bfloat16 [2048, 4096], P('group', 'expert'), may hold values from -14 to 14
- self_latent: bfloat16 [2048, 512], P('group'), may hold values from -4 to 4
- self_rope: bfloat16 [2048, 64], P('group'), may hold values from -4 to 4
- cache_latent: bfloat16 [8, 512, 512], P('group'), may hold values from -4 to 4
- cache_rope: bfloat16 [8, 64, 512], P('group'), may hold values from -4 to 4
- prompt_of_sample: int32 [2048], P('group'), may hold values from 0 to 7, as said below
- w_uv: bfloat16 [64, 512, 128], P('expert'), may hold values from -0.25 to 0.25
- w_out: bfloat16 [8192, 7168], P('expert'), may hold values from -0.0625 to 0.0625
- residual: bfloat16 [2048, 7168], P(('group', 'expert')), may hold values from -40 to 40
- norm_gain: float32 [7168], replicated, may hold values from 0.1 to 1.9
- expert_ids: int32 [2048, 8], P(('group', 'expert')), may hold values from 0 to 31, all different within a row; in each aligned block of 8 rows (0 to 7, 8 to 15, ...) at most 3 rows name the same one
- gate_weight: float32 [2048, 8], P(('group', 'expert')), may hold values from 0.1 to 0.6
- w_gate: bfloat16 [32, 7168, 1024], P('expert', 'group'), may hold values from -0.0625 to 0.0625
- w_up: bfloat16 [32, 7168, 1024], P('expert', 'group'), may hold values from -0.0625 to 0.0625
- w_down: bfloat16 [32, 1024, 7168], P('expert', None, 'group'), may hold values from -0.1875 to 0.1875
Outputs:
- attn_proj: bfloat16 [2048, 7168], P(('group', 'expert'))
- moe_out: bfloat16 [2048, 7168], P(('group', 'expert'))
The draws below stay inside these ranges and needn't reach their ends.
Inputs may be any that keep to these rules, and one draw needn't show every extreme that they name: `expert_ids`: in the rows of one device, each expert is named at most 3 times. `prompt_of_sample`: the 256 samples of each sample group form 8 * 4 consecutive blocks of equal size; all samples of a block share one prompt, and each prompt owns exactly 4 blocks of each group.
All inputs are finite; a program needn't handle non-finite values.
Results may differ from the reference program's by a relative error of at most 0.04.
Values may be sent and summed in bfloat16 or wider, within the bound.
No kernel may reach another device: no remote copies, remote signals or barrier semaphores. Data moves between devices by JAX's collectives and lax.ppermute only.
A program may use at most 64 MiB of HBM per device.

```python
import math
import jax
import jax.numpy as jnp
import numpy as np
from jax import lax

D = 7168
HEADS = 64
LAT = 512
ROPE = 64
VD = 128
FFE = 1024
TOP = 8
RUNS = 4
LEN = 512
SAMP_DEV = 8
SAMP_GRP = 256
SAMPLES = 2048
EXPERTS = 32
CAP = 3
N_GROUP = 8


def shared_parts(key):
    base_key = jax.random.fold_in(key, 1000)
    key_dir = jax.random.fold_in(base_key, 0)
    direction = jnp.clip(jax.random.normal(key_dir, (SAMPLES, ROPE), jnp.float32), -4.0, 4.0)
    return direction


def draw_q_latent(key, part):
    key = jax.random.fold_in(key, 3)
    values = jnp.clip(jax.random.normal(key, (SAMPLES, HEADS, LAT), jnp.float32), -4.0, 4.0)
    return values.astype(jnp.bfloat16)


def draw_q_rope(key, part):
    direction = shared_parts(key)
    key = jax.random.fold_in(key, 5)
    noise = jnp.clip(jax.random.normal(key, (SAMPLES, HEADS, ROPE), jnp.float32), -4.0, 4.0)
    values = 2.0 * direction[:, None, :] + noise
    return values.reshape(SAMPLES, HEADS * ROPE).astype(jnp.bfloat16)


def draw_self_rope(key, part):
    direction = shared_parts(key)
    return direction.astype(jnp.bfloat16)


def draw_cache_rope(key, part):
    key = jax.random.fold_in(key, 9)
    key_vals = jax.random.fold_in(key, 0)
    values = jnp.clip(jax.random.normal(key_vals, (N_GROUP, ROPE, LEN), jnp.float32), -4.0, 4.0)
    return values.astype(jnp.bfloat16)


def draw_prompt_of_sample(key, part):
    key = jax.random.fold_in(key, 13)
    group_keys = jax.random.split(key, N_GROUP)
    base = jnp.repeat(jnp.arange(N_GROUP, dtype=jnp.int32), RUNS)
    orders = jax.vmap(lambda one_key: jax.random.permutation(one_key, base))(group_keys).astype(jnp.int32)
    block_size = SAMP_GRP // (N_GROUP * RUNS)
    return jnp.repeat(orders, block_size, axis=1).reshape(SAMPLES).astype(jnp.int32)


def draw_residual(key, part):
    key = jax.random.fold_in(key, 11)
    key_rows, key_cols, key_vals = jax.random.split(key, 3)
    row_scale = jnp.exp(jax.random.uniform(key_rows, (SAMPLES, 1), jnp.float32, math.log(0.3), math.log(3.0)))
    col_scale = jnp.exp(jax.random.uniform(key_cols, (1, D), jnp.float32, math.log(0.3), math.log(3.0)))
    values = jnp.clip(jax.random.normal(key_vals, (SAMPLES, D), jnp.float32), -4.0, 4.0)
    return jnp.clip(values * row_scale * col_scale, -40.0, 40.0).astype(jnp.bfloat16)


def shard_levels(stream_key, dims, pieces, smallest, high):
    level = 1.0
    for dim, blocks in pieces:
        heights = jax.random.uniform(jax.random.fold_in(jax.random.fold_in(stream_key, 6), dim), (blocks,), jnp.float32, smallest / len(pieces), high / len(pieces))
        level = level * jnp.repeat(jnp.exp(heights), dims[dim] // blocks).reshape((-1,) + (1,) * (len(dims) - 1 - dim))
    return level


def routed_block(rng, own, number, rows, count, top, reach, skew):
    order = jax.random.permutation(rng, count)
    heavy_load, ordinary = portions_of(count, rows * top, reach, skew, True), portions_of(count, rows * top, reach, skew, False)
    places = jnp.arange(count)

    def named(tallies, rotation):
        used = int((tallies > 0).sum())
        fixed = max(1, used // 4)
        shifted = fixed + (places - fixed + rotation * (used - fixed)) % max(1, count - fixed)
        return jnp.zeros((count,), jnp.int32).at[order[jnp.where(places < fixed, places, shifted)]].set(jnp.asarray(tallies, jnp.int32))

    tallies = jnp.where(number % 4 == 0, named(heavy_load, number // 4), named(ordinary, number - number // 4 - 1))
    mixed = jax.random.permutation(jax.random.fold_in(own, 3), count)
    donor, taker = mixed[0:count // 2 * 2:2], mixed[1:count // 2 * 2:2]
    room = jnp.minimum(tallies[donor] - 1, reach - tallies[taker]) // 2
    room = jnp.where((donor == order[0]) | (taker == order[0]) | (tallies[taker] == 0), 0, jnp.maximum(room, 0))
    shifted = jax.random.randint(jax.random.fold_in(own, 4), (count // 2,), 0, 1 << 20) % (room + 1)
    tallies = tallies.at[donor].add(-shifted).at[taker].add(shifted)
    items = jnp.searchsorted(jnp.cumsum(tallies), jnp.arange(rows * top), side="right").astype(jnp.int32)
    table = items.reshape(top, rows).T
    table = table[jax.random.permutation(jax.random.fold_in(own, 1), rows)]
    rotation = jax.random.randint(jax.random.fold_in(own, 2), (rows, 1), 0, top)
    return jnp.take_along_axis(table, (jnp.arange(top)[None, :] + rotation) % top, axis=1)


def portions_of(amount, total, limit, slope, full):
    weights = [(1 << 20) // math.isqrt(standing ** slope) + 1 for standing in range(1, amount + 1)]
    largest = limit if full else min(limit, max(-(-total // amount), total * weights[0] // sum(weights)))
    least = 1 if total - largest >= amount - 1 else 0
    holding, spare = [largest] + [least] * (amount - 1), total - largest - least * (amount - 1)
    while spare > 0:
        free = [i for i in range(1, amount) if holding[i] < largest] or [i for i in range(1, amount) if holding[i] < limit]
        pool, budget = sum([weights[i] for i in free]), spare
        for i in free:
            extra = min(limit - holding[i], max(1, budget * weights[i] // pool), spare)
            holding[i] = holding[i] + extra
            spare = spare - extra
    return np.array(holding)


def normal_values(own_key, shape, deviation, most, pieces=(), kind=jnp.bfloat16):
    gain = shard_levels(own_key, shape, pieces, -0.22, 0.18) if pieces else 1.0
    entries = jax.random.normal(own_key, shape, jnp.float32) * deviation * gain
    return jnp.minimum(jnp.maximum(entries, -most), most).astype(kind)


def setup_inputs(seed: int = 0) -> dict:
    splits = jax.random.split(jax.random.key(seed), 17)
    q_latent = draw_q_latent(jax.random.fold_in(splits[16], 71), 0)
    q_rope = draw_q_rope(jax.random.fold_in(splits[16], 71), 0)
    self_latent = normal_values(splits[2], (SAMPLES, LAT), 1.0, 4.0, ((0, 8),))
    self_rope = draw_self_rope(jax.random.fold_in(splits[16], 71), 0)
    cache_latent = normal_values(splits[4], (N_GROUP, LEN, LAT), 1.0, 4.0, ((0, 8),))
    cache_rope = draw_cache_rope(jax.random.fold_in(splits[16], 71), 0)
    prompt_of_sample = draw_prompt_of_sample(jax.random.fold_in(splits[16], 71), 0)
    w_uv = normal_values(splits[7], (HEADS, LAT, VD), LAT ** -0.5, 0.25, ((0, 32),))
    w_out = normal_values(splits[8], (HEADS * VD, D), (HEADS * VD) ** -0.5, 0.0625, ((0, 32),))
    residual = draw_residual(jax.random.fold_in(splits[16], 71), 0)
    norm_gain = jnp.clip(1.0 + 0.18 * jax.random.normal(splits[10], (D,), jnp.float32), 0.1, 1.9)
    expert_ids_keys = jax.random.split(jax.random.fold_in(splits[11], 1), SAMPLES // SAMP_DEV)
    expert_ids_turns = jax.random.permutation(jax.random.fold_in(splits[11], 3), SAMPLES // SAMP_DEV)
    expert_ids = jax.vmap(lambda own, number: routed_block(jax.random.fold_in(splits[11], 2), own, number, SAMP_DEV, EXPERTS, TOP, CAP, 1))(expert_ids_keys, expert_ids_turns).reshape((SAMPLES, TOP))
    gate_weight = jnp.clip(0.1 + 0.5 * jax.random.uniform(splits[12], (SAMPLES, TOP), jnp.float32) ** shard_levels(splits[12], (SAMPLES, TOP), ((0, 256),), -0.2, 0.2), 0.1, 0.6)
    w_gate = normal_values(splits[13], (EXPERTS, D, FFE), D ** -0.5, 0.0625, ((0, 32), (1, 8)))
    w_up = normal_values(splits[14], (EXPERTS, D, FFE), D ** -0.5, 0.0625, ((0, 32), (1, 8)))
    w_down = normal_values(splits[15], (EXPERTS, FFE, D), FFE ** -0.5, 0.1875, ((0, 32), (2, 8)))
    return dict(q_latent=q_latent, q_rope=q_rope, self_latent=self_latent, self_rope=self_rope, cache_latent=cache_latent, cache_rope=cache_rope, prompt_of_sample=prompt_of_sample, w_uv=w_uv, w_out=w_out, residual=residual, norm_gain=norm_gain, expert_ids=expert_ids, gate_weight=gate_weight, w_gate=w_gate, w_up=w_up, w_down=w_down)


NORM_EPS = 1e-06

def reference(q_latent, q_rope, self_latent, self_rope, cache_latent, cache_rope, prompt_of_sample, w_uv, w_out, residual, norm_gain, expert_ids, gate_weight, w_gate, w_up, w_down):
    score_scale = (VD + ROPE) ** (-0.5)
    blocks = SAMPLES // SAMP_DEV
    inputs = (q_latent.reshape(blocks, SAMP_DEV, HEADS, LAT), q_rope.reshape(blocks, SAMP_DEV, HEADS, ROPE), self_latent.reshape(blocks, SAMP_DEV, LAT), self_rope.reshape(blocks, SAMP_DEV, ROPE), prompt_of_sample.reshape(blocks, SAMP_DEV))
    w_uv_wide = w_uv.astype(jnp.float32)

    def attend_block(block_args):
        q_lat, q_pos, self_lat, self_pos, prompt = block_args
        keys_lat = cache_latent[prompt].astype(jnp.float32)
        keys_pos = cache_rope[prompt].astype(jnp.float32)
        q_lat_wide = q_lat.astype(jnp.float32)
        q_pos_wide = q_pos.astype(jnp.float32)
        self_wide = self_lat.astype(jnp.float32)
        scores = (jnp.einsum('bhc,btc->bht', q_lat_wide, keys_lat) + jnp.einsum('bhr,brt->bht', q_pos_wide, keys_pos)) * score_scale
        self_scores = (jnp.einsum('bhc,bc->bh', q_lat_wide, self_wide) + jnp.einsum('bhr,br->bh', q_pos_wide, self_pos.astype(jnp.float32))) * score_scale
        top_score = jnp.maximum(lax.optimization_barrier(jnp.max(scores, axis=-1)), self_scores)
        weights = jnp.exp(scores - top_score[..., None])
        self_weight = jnp.exp(self_scores - top_score)
        totals = lax.optimization_barrier(jnp.sum(weights, axis=-1)) + self_weight
        weights_b = lax.optimization_barrier(weights.astype(jnp.bfloat16)).astype(jnp.float32)
        self_b = lax.optimization_barrier(self_weight.astype(jnp.bfloat16)).astype(jnp.float32)
        summed = jnp.einsum('bht,btc->bhc', weights_b, keys_lat) + self_b[..., None] * self_wide[:, None, :]
        latent_out = lax.optimization_barrier((summed / totals[..., None]).astype(jnp.bfloat16))
        head_value = jnp.einsum('bhc,hcv->bhv', latent_out.astype(jnp.float32), w_uv_wide).astype(jnp.bfloat16)
        return head_value.reshape(SAMP_DEV, HEADS * VD)
    values = lax.map(attend_block, inputs).reshape(SAMPLES, HEADS * VD)
    attn_proj = jnp.dot(values, w_out, preferred_element_type=jnp.float32).astype(jnp.bfloat16)
    mixed = residual.astype(jnp.float32) + lax.optimization_barrier(attn_proj).astype(jnp.float32)
    normed = (mixed * lax.rsqrt(lax.optimization_barrier(jnp.mean(mixed * mixed, axis=-1, keepdims=True)) + NORM_EPS) * norm_gain).astype(jnp.bfloat16)
    devices = SAMPLES // SAMP_DEV
    pair_ids = expert_ids.reshape(devices, SAMP_DEV * TOP)
    onehot = (pair_ids[..., None] == jnp.arange(EXPERTS, dtype=jnp.int32)).astype(jnp.int32)
    earlier = jnp.cumsum(onehot, axis=1) - onehot
    slot_of = lax.optimization_barrier(jnp.sum(earlier * onehot, axis=-1)).astype(jnp.int32)
    source = jnp.broadcast_to(jnp.arange(devices, dtype=jnp.int32)[:, None], slot_of.shape)
    token = source * SAMP_DEV + jnp.arange(SAMP_DEV * TOP, dtype=jnp.int32)[None, :] // TOP
    table = jnp.full((EXPERTS, devices, CAP), SAMPLES, jnp.int32).at[pair_ids, source, slot_of].set(token)
    padded = jnp.concatenate([normed, jnp.zeros((1, D), jnp.bfloat16)], axis=0)
    share = D // N_GROUP

    def run_expert(args):
        rows_index, gate_w, up_w, down_w = args
        rows = padded[rows_index.reshape(-1)].astype(jnp.float32).reshape(-1, N_GROUP, share)
        gate_parts = jnp.einsum('rgd,gdf->grf', rows, gate_w.astype(jnp.float32).reshape(N_GROUP, share, FFE))
        up_parts = jnp.einsum('rgd,gdf->grf', rows, up_w.astype(jnp.float32).reshape(N_GROUP, share, FFE))
        gate_val = lax.optimization_barrier(jnp.sum(lax.optimization_barrier(gate_parts.astype(jnp.bfloat16)).astype(jnp.float32), axis=0))
        up_val = lax.optimization_barrier(jnp.sum(lax.optimization_barrier(up_parts.astype(jnp.bfloat16)).astype(jnp.float32), axis=0))
        hidden = (jax.nn.silu(gate_val) * up_val).astype(jnp.bfloat16)
        return jnp.dot(hidden, down_w, preferred_element_type=jnp.float32).astype(jnp.bfloat16)
    expert_rows = lax.map(run_expert, (table, w_gate, w_up, w_down))
    flat_rows = lax.optimization_barrier(expert_rows.reshape(EXPERTS * devices * CAP, D))
    where_row = ((pair_ids * devices + source) * CAP + slot_of).reshape(SAMPLES, TOP)
    moe = jnp.zeros((SAMPLES, D), jnp.float32)
    for pick in range(TOP):
        moe = moe + gate_weight[:, pick:pick + 1] * flat_rows[where_row[:, pick]].astype(jnp.float32)
    return (attn_proj, moe.astype(jnp.bfloat16))
```

```python
import jax
import jax.numpy as jnp
from jax import lax
from jax.sharding import Mesh, PartitionSpec as P

ROPE = 64
VD = 128
NORM_EPS = 1e-06
RUNS = 4
CAP = 3

GROUP = ("zlo", "core")
XY = ("x", "y")
BF = jnp.bfloat16
F32 = jnp.float32


def dot(a, b):
    return jnp.dot(a, b, preferred_element_type=F32)


def dot_t(a, b):
    return lax.dot_general(a, b, (((1,), (1,)), ((), ())), preferred_element_type=F32)


def split3(value):
    one = value.astype(BF)
    rest = value - one.astype(F32)
    two = rest.astype(BF)
    three = (rest - two.astype(F32)).astype(BF)
    return one, two, three


def exchange(value, axes):
    return lax.all_to_all(value, axes, 0, 0, tiled=True)


def block_permutation(prompt_of_sample, prompts):
    samples = prompt_of_sample.shape[0]
    block = samples // (prompts * RUNS)
    own = prompt_of_sample.reshape(-1, block)[:, 0]
    blocks = own.shape[0]
    at = jnp.arange(blocks, dtype=jnp.int32)
    same = (own[:, None] == own[None, :]) & (at[None, :] < at[:, None])
    rank = own * RUNS + jnp.sum(same.astype(jnp.int32), axis=1)
    rank_of_sample = jnp.repeat(rank, block) * block + jnp.arange(samples, dtype=jnp.int32) % block
    return rank_of_sample


def body(
    q_latent,
    q_rope,
    self_latent,
    self_rope,
    cache_latent,
    cache_rope,
    prompt_of_sample,
    w_uv,
    w_out,
    residual,
    norm_gain,
    expert_ids,
    gate_weight,
    w_gate,
    w_up,
    w_down,
):
    groups = lax.axis_size(GROUP)
    halves = lax.axis_size("zhi")
    planes = lax.axis_size(XY)
    my_half = lax.axis_index("zhi")
    my_core = lax.axis_index("core")
    samples, heads, lat = q_latent.shape
    experts = planes * halves
    rows_here = residual.shape[0]
    width = residual.shape[1]
    share = width // groups
    scale = (VD + ROPE) ** (-0.5)

    table = jnp.concatenate([expert_ids.astype(F32), gate_weight], axis=1)
    table = lax.all_gather(table, GROUP + ("zhi",), axis=0, tiled=True)
    tokens = table.shape[0]
    top = expert_ids.shape[1]
    ids = table[:, :top].astype(jnp.int32)
    gates = table[:, top:]
    wanted = jnp.arange(planes, dtype=jnp.int32) * halves + my_half
    hit = ids[:, :, None] == wanted[None, None, :]
    member = jnp.any(hit, axis=1)
    gate_of = jnp.sum(jnp.where(hit, gates[:, :, None], 0.0), axis=1)
    before = jnp.cumsum(member.astype(jnp.int32), axis=0) - member.astype(jnp.int32)
    slots = tokens // rows_here * CAP
    place = jnp.where(member, before, -1).T
    routed = place[:, None, :] == jnp.arange(slots, dtype=jnp.int32)[None, :, None]
    routing = routed.reshape(planes * slots, tokens).astype(BF)
    weights = jnp.where(routed, gate_of.T[:, None, :], 0.0).reshape(planes * slots, tokens)
    gate_hi = weights.astype(BF)
    gate_lo = (weights - gate_hi.astype(F32)).astype(BF)

    rank = block_permutation(prompt_of_sample, groups)
    to_rank = (rank[None, :] == jnp.arange(samples, dtype=jnp.int32)[:, None]).astype(BF)
    q_all = jnp.concatenate([q_latent.reshape(samples, heads * lat), q_rope], axis=1)
    q_sorted = dot(to_rank, q_all).astype(BF)
    q_here = exchange(q_sorted, GROUP)
    keys = cache_latent[0]
    rope_keys = cache_rope[0]
    outs = []
    stats = []
    for head in range(heads):
        q_head = q_here[:, head * lat : (head + 1) * lat]
        r_head = q_here[:, heads * lat + head * ROPE : heads * lat + (head + 1) * ROPE]
        score = (dot_t(q_head, keys) + dot(r_head, rope_keys)) * scale
        best = jnp.max(score, axis=-1, keepdims=True)
        weight = jnp.exp(score - best)
        total = jnp.sum(weight, axis=-1, keepdims=True)
        latent = (dot(weight.astype(BF), keys) / total).astype(BF)
        outs.append(dot(latent, w_uv[head]).astype(BF))
        stats.extend(split3(best + jnp.log(total)))
    pad = jnp.zeros((samples, VD - len(stats)), BF)
    back = exchange(jnp.concatenate(outs + stats + [pad], axis=1), GROUP)
    back = lax.dot_general(to_rank, back, (((0,), (0,)), ((), ())), preferred_element_type=F32)
    values = []
    self_wide = self_latent.astype(F32)
    for head in range(heads):
        self_score = (
            jnp.sum(q_latent[:, head].astype(F32) * self_wide, axis=-1, keepdims=True)
            + jnp.sum(
                q_rope[:, head * ROPE : (head + 1) * ROPE].astype(F32) * self_rope.astype(F32),
                axis=-1,
                keepdims=True,
            )
        ) * scale
        at = heads * VD + 3 * head
        lse = back[:, at : at + 1] + back[:, at + 1 : at + 2] + back[:, at + 2 : at + 3]
        best = jnp.maximum(lse, self_score)
        cache_part = jnp.exp(lse - best)
        self_part = jnp.exp(self_score - best)
        own_value = dot(self_latent, w_uv[head])
        mixed_value = cache_part * back[:, head * VD : (head + 1) * VD] + self_part * own_value
        values.append((mixed_value / (cache_part + self_part)).astype(BF))
    head_value = jnp.concatenate(values, axis=1)

    partial = dot(head_value, w_out).astype(BF)
    arrived = exchange(partial, XY).reshape(planes, halves * rows_here, width)
    near = jnp.sum(arrived.astype(F32), axis=0).reshape(halves, rows_here, width)
    is_mine = (jnp.arange(halves) == my_half)[:, None, None]
    with_residual = near + jnp.where(is_mine, residual.astype(F32)[None], 0.0)
    far = lax.ppermute(with_residual.astype(BF), "zhi", [(0, 1), (1, 0)]).astype(F32)
    attn_proj = lax.dynamic_index_in_dim(near + far, my_half, 0, keepdims=False).astype(BF)
    mixed = with_residual + far
    normed = (
        mixed * lax.rsqrt(jnp.mean(mixed * mixed, axis=-1, keepdims=True) + NORM_EPS) * norm_gain
    ).astype(BF)

    by_block = normed.reshape(halves * rows_here, groups, share).transpose(1, 0, 2)
    token_rows = exchange(by_block, GROUP).reshape(tokens, share)
    rows_in = exchange(dot(routing, token_rows).astype(BF), XY)

    half_rows = rows_in.shape[0] // 2
    w_both = (w_gate[0], w_up[0])

    def both(rows):
        return jnp.concatenate([dot(rows, w).astype(BF) for w in w_both], axis=1)

    other_rows = lax.dynamic_slice_in_dim(rows_in, (1 - my_core) * half_rows, half_rows, 0)
    own_rows = lax.dynamic_slice_in_dim(rows_in, my_core * half_rows, half_rows, 0)
    from_core = lax.ppermute(both(other_rows), "core", [(0, 1), (1, 0)])
    chip_sum = (both(own_rows).astype(F32) + from_core.astype(F32)).astype(BF)
    lines = lax.axis_size("zlo")
    parts = exchange(chip_sum, "zlo").reshape(lines, half_rows // lines, -1)
    sums = jnp.sum(parts.astype(F32), axis=0)
    ffe = sums.shape[1] // 2
    hidden = (jax.nn.silu(sums[:, :ffe]) * sums[:, ffe:]).astype(BF)
    hidden = lax.all_gather(hidden, ("core", "zlo"), axis=0, tiled=True)
    expert_out = dot(hidden, w_down[0]).astype(BF)

    returned = exchange(expert_out, XY)
    over_rows = (((0,), (0,)), ((), ()))
    moe = lax.dot_general(gate_hi, returned, over_rows, preferred_element_type=F32)
    moe = moe + lax.dot_general(gate_lo, returned, over_rows, preferred_element_type=F32)
    moe = exchange(moe.astype(BF), GROUP + ("zhi",))
    moe = jnp.sum(moe.reshape(groups, halves, rows_here, share).astype(F32), axis=1).astype(BF)
    moe_out = moe.transpose(1, 0, 2).reshape(rows_here, width)
    return (attn_proj, moe_out)


def solution(mesh):
    fine = Mesh(mesh.devices.reshape(4, 2, 4, 4, 2), ("zlo", "core", "x", "y", "zhi"))
    g = GROUP
    e = XY + ("zhi",)
    in_specs = (
        P(g, e, None),
        P(g, e),
        P(g, None),
        P(g, None),
        P(g, None, None),
        P(g, None, None),
        P(g),
        P(e, None, None),
        P(e, None),
        P(g + e, None),
        P(),
        P(g + e, None),
        P(g + e, None),
        P(e, g, None),
        P(e, g, None),
        P(e, None, g),
    )
    out_specs = (P(g + e, None), P(g + e, None))
    return jax.shard_map(body, mesh=fine, in_specs=in_specs, out_specs=out_specs, check_vma=False)
```

```python
import jax
import jax.numpy as jnp
from jax import lax
from jax.sharding import Mesh, PartitionSpec as P

ROPE = 64
VD = 128
NORM_EPS = 1e-06
RUNS = 4
CAP = 3
ROWS = 8
CHUNKS = 1
GATHER = "sc"

GROUP = ("zlo", "core")
XY = ("x", "y")
BF = jnp.bfloat16
F32 = jnp.float32


def dot(a, b):
    return jnp.dot(a, b, preferred_element_type=F32)


def dot_t(a, b):
    return lax.dot_general(a, b, (((1,), (1,)), ((), ())), preferred_element_type=F32)


def split3(value):
    one = value.astype(BF)
    rest = value - one.astype(F32)
    two = rest.astype(BF)
    three = (rest - two.astype(F32)).astype(BF)
    return one, two, three


def exchange(value, axes):
    return lax.all_to_all(value, axes, 0, 0, tiled=True)


def block_permutation(prompt_of_sample, prompts):
    samples = prompt_of_sample.shape[0]
    block = samples // (prompts * RUNS)
    own = prompt_of_sample.reshape(-1, block)[:, 0]
    blocks = own.shape[0]
    at = jnp.arange(blocks, dtype=jnp.int32)
    same = (own[:, None] == own[None, :]) & (at[None, :] < at[:, None])
    rank = own * RUNS + jnp.sum(same.astype(jnp.int32), axis=1)
    rank_of_sample = jnp.repeat(rank, block) * block + jnp.arange(samples, dtype=jnp.int32) % block
    return rank_of_sample


SIDE = 4
LINES = 4
CORES = 2
HALVES = 2
ALL = ("zlo", "core", "x", "y", "zhi")


def shift(count, k):
    return [(i, (i + k) % count) for i in range(count)]


def sum_wide(parts):
    total = parts[0].astype(F32)
    for part in parts[1:]:
        total = total + part.astype(F32)
    return total


def plane_shift(k, stage):
    pairs = []
    sizes = (LINES, CORES, SIDE, SIDE, HALVES)

    def number(place):
        flat = 0
        for size, one in zip(sizes, place):
            flat = flat * size + one
        return flat

    for flat in range(LINES * CORES * SIDE * SIDE * HALVES):
        place, rest = [], flat
        for size in reversed(sizes):
            place.insert(0, rest % size)
            rest //= size
        there = list(place)
        axis = 2 if place[1] == stage else 3
        there[axis] = (there[axis] + k) % SIDE
        pairs.append((number(place), number(there)))
    return pairs


def plane_order(my_core):
    me = (lax.axis_index("x"), lax.axis_index("y"))
    count = SIDE * SIDE * HALVES * ROWS
    row = jnp.arange(count, dtype=jnp.int32)
    rest = row % (HALVES * ROWS)
    first = row // (HALVES * ROWS) // SIDE
    second = row // (HALVES * ROWS) % SIDE
    x = (me[0] + jnp.where(my_core == 0, first, second)) % SIDE
    y = (me[1] + jnp.where(my_core == 0, second, first)) % SIDE
    source = (x * SIDE + y) * (HALVES * ROWS) + rest
    return (source[:, None] == row[None, :]).astype(BF)


def body(
    q_latent,
    q_rope,
    self_latent,
    self_rope,
    cache_latent,
    cache_rope,
    prompt_of_sample,
    w_uv,
    w_out,
    residual,
    norm_gain,
    expert_ids,
    gate_weight,
    w_gate,
    w_up,
    w_down,
):
    groups = lax.axis_size(GROUP)
    halves = lax.axis_size("zhi")
    planes = lax.axis_size(XY)
    my_half = lax.axis_index("zhi")
    my_core = lax.axis_index("core")
    samples, heads, lat = q_latent.shape
    experts = planes * halves
    rows_here = residual.shape[0]
    width = residual.shape[1]
    share = width // groups
    scale = (VD + ROPE) ** (-0.5)

    top = expert_ids.shape[1]
    tokens = groups * halves * rows_here
    own_table = jnp.concatenate([expert_ids.astype(BF), *split3(gate_weight)], axis=1)
    other_table = lax.ppermute(own_table, "zhi", [(0, 1), (1, 0)])
    table = jnp.concatenate(
        [
            jnp.where(my_half == 0, own_table, other_table),
            jnp.where(my_half == 0, other_table, own_table),
        ],
        axis=0,
    )

    rank = block_permutation(prompt_of_sample, groups)
    to_rank = (rank[None, :] == jnp.arange(samples, dtype=jnp.int32)[:, None]).astype(BF)
    q_all = jnp.concatenate([q_latent.reshape(samples, heads * lat), q_rope], axis=1)
    q_sorted = dot(to_rank, q_all).astype(BF)
    q_here = exchange(q_sorted, GROUP)
    keys = cache_latent[0]
    rope_keys = cache_rope[0]
    outs = []
    stats = []
    for head in range(heads):
        q_head = q_here[:, head * lat : (head + 1) * lat]
        r_head = q_here[:, heads * lat + head * ROPE : heads * lat + (head + 1) * ROPE]
        score = (dot_t(q_head, keys) + dot(r_head, rope_keys)) * scale
        best = jnp.max(score, axis=-1, keepdims=True)
        weight = jnp.exp(score - best)
        total = jnp.sum(weight, axis=-1, keepdims=True)
        latent = (dot(weight.astype(BF), keys) / total).astype(BF)
        outs.append(dot(latent, w_uv[head]).astype(BF))
        stats.extend(split3(best + jnp.log(total)))
    pad = jnp.zeros((samples, VD - len(stats) - table.shape[1]), BF)
    table = jnp.pad(table, ((0, samples // groups - table.shape[0]), (0, 0)))
    table = jnp.tile(table, (groups, 1))
    back = exchange(jnp.concatenate(outs + stats + [table, pad], axis=1), GROUP)

    table = back.reshape(groups, samples // groups, -1)[:, : halves * rows_here]
    table = table[:, :, heads * VD + len(stats) :].reshape(tokens, -1).astype(F32)
    ids = table[:, :top].astype(jnp.int32)
    gates = table[:, top : 2 * top] + table[:, 2 * top : 3 * top] + table[:, 3 * top : 4 * top]
    wanted = jnp.arange(planes, dtype=jnp.int32) * halves + my_half
    slots = tokens // rows_here * CAP // CHUNKS
    tables = []
    for chunk in range(CHUNKS):
        some_ids = ids.reshape(groups, CHUNKS, -1, top)[:, chunk].reshape(-1, top)
        some_gates = gates.reshape(groups, CHUNKS, -1, top)[:, chunk].reshape(-1, top)
        hit = some_ids[:, :, None] == wanted[None, None, :]
        member = jnp.any(hit, axis=1)
        gate_of = jnp.sum(jnp.where(hit, some_gates[:, :, None], 0.0), axis=1)
        before = jnp.cumsum(member.astype(jnp.int32), axis=0) - member.astype(jnp.int32)
        place = jnp.where(member, before, -1).T
        routed = place[:, None, :] == jnp.arange(slots, dtype=jnp.int32)[None, :, None]
        routed = routed.reshape(planes * slots, -1)
        weights = jnp.where(routed, jnp.repeat(gate_of.T, slots, axis=0), 0.0)
        gate_hi = weights.astype(BF)
        tables.append((routed.astype(BF), gate_hi, (weights - gate_hi.astype(F32)).astype(BF)))

    back = lax.dot_general(to_rank, back, (((0,), (0,)), ((), ())), preferred_element_type=F32)
    values = []
    self_wide = self_latent.astype(F32)
    for head in range(heads):
        self_score = (
            jnp.sum(q_latent[:, head].astype(F32) * self_wide, axis=-1, keepdims=True)
            + jnp.sum(
                q_rope[:, head * ROPE : (head + 1) * ROPE].astype(F32) * self_rope.astype(F32),
                axis=-1,
                keepdims=True,
            )
        ) * scale
        at = heads * VD + 3 * head
        lse = back[:, at : at + 1] + back[:, at + 1 : at + 2] + back[:, at + 2 : at + 3]
        best = jnp.maximum(lse, self_score)
        cache_part = jnp.exp(lse - best)
        self_part = jnp.exp(self_score - best)
        own_value = dot(self_latent, w_uv[head])
        mixed_value = cache_part * back[:, head * VD : (head + 1) * VD] + self_part * own_value
        values.append((mixed_value / (cache_part + self_part)).astype(BF))
    head_value = jnp.concatenate(values, axis=1)

    head_rows = dot(plane_order(my_core), head_value).astype(BF)
    near = [None] * CHUNKS
    block = halves * rows_here // CHUNKS
    for chunk in range(CHUNKS):
        rows = head_rows.reshape(SIDE, SIDE, CHUNKS, block, -1)[:, :, chunk]
        first = [dot(rows[k].reshape(SIDE * block, -1), w_out).astype(BF) for k in range(SIDE)]
        first = sum_wide(first[:1] + [lax.ppermute(first[k], ALL, plane_shift(k, 0)) for k in (2, 1, 3)])
        first = first.astype(BF).reshape(SIDE, block, width)
        near[chunk] = sum_wide(
            [first[0]] + [lax.ppermute(first[k], ALL, plane_shift(k, 1)) for k in (2, 1, 3)]
        )

    moes = []
    projections = []
    for chunk in range(CHUNKS):
        part = near[chunk].reshape(halves // CHUNKS, rows_here, width)
        is_mine = (jnp.arange(halves // CHUNKS) + chunk * (halves // CHUNKS) == my_half)[:, None, None]
        with_residual = part + jnp.where(is_mine, residual.astype(F32)[None], 0.0)
        far = lax.ppermute(with_residual.astype(BF), "zhi", [(0, 1), (1, 0)]).astype(F32)
        projections.append(part + far)
        mixed = with_residual + far
        normed = (
            mixed * lax.rsqrt(jnp.mean(mixed * mixed, axis=-1, keepdims=True) + NORM_EPS) * norm_gain
        ).astype(BF)

        by_block = normed.reshape(block, groups, share).transpose(1, 0, 2)
        token_rows = exchange(by_block, GROUP).reshape(tokens // CHUNKS, share)
        routing, gate_hi, gate_lo = tables[chunk]
        rows_in = exchange(dot(routing, token_rows).astype(BF), XY)

        half_rows = rows_in.shape[0] // 2

        def both(rows):
            return jnp.concatenate([dot(rows, w_gate[0]).astype(BF), dot(rows, w_up[0]).astype(BF)], axis=1)

        other_rows = lax.dynamic_slice_in_dim(rows_in, (1 - my_core) * half_rows, half_rows, 0)
        own_rows = lax.dynamic_slice_in_dim(rows_in, my_core * half_rows, half_rows, 0)
        from_core = lax.ppermute(both(other_rows), "core", [(0, 1), (1, 0)])
        own = both(own_rows)
        lines = lax.axis_size("zlo")
        line_rows = half_rows // lines
        my_line = lax.axis_index("zlo")
        parts = []
        for k in (2, 1, 3, 0):
            at = (my_line + k) % lines * line_rows
            here = lax.dynamic_slice_in_dim(own, at, line_rows, 0).astype(F32)
            here = here + lax.dynamic_slice_in_dim(from_core, at, line_rows, 0).astype(F32)
            parts.append(lax.ppermute(here.astype(BF), "zlo", shift(lines, k)) if k else here)
        sums = sum_wide(parts)
        ffe = sums.shape[1] // 2
        hidden = (jax.nn.silu(sums[:, :ffe]) * sums[:, ffe:]).astype(BF)
        if GATHER == "sc":
            mine = lax.all_gather(hidden, "zlo", axis=0, tiled=True)
        else:
            got = [hidden] + [lax.ppermute(hidden, "zlo", shift(lines, k)) for k in (1, 2, 3)]
            mine = jnp.concatenate(got, axis=0)
        theirs = lax.ppermute(mine, "core", [(0, 1), (1, 0)])
        down = [dot(mine, w_down[0]).astype(BF), dot(theirs, w_down[0]).astype(BF)]
        if GATHER == "sc":
            order = [jnp.where(my_core == 0, down[0], down[1]), jnp.where(my_core == 0, down[1], down[0])]
            expert_out = jnp.concatenate(order, axis=0)
        else:
            expert_out = jnp.zeros((2 * half_rows, share), BF)
            for side in range(2):
                base = (my_core if side == 0 else 1 - my_core) * half_rows
                for k in range(lines):
                    at = base + (my_line - k) % lines * line_rows
                    expert_out = lax.dynamic_update_slice_in_dim(
                        expert_out, down[side][k * line_rows : (k + 1) * line_rows], at, 0
                    )

        returned = exchange(expert_out, XY)
        over_rows = (((0,), (0,)), ((), ()))
        moe = lax.dot_general(gate_hi, returned, over_rows, preferred_element_type=F32)
        moe = moe + lax.dot_general(gate_lo, returned, over_rows, preferred_element_type=F32)
        moes.append(moe.astype(BF).reshape(groups, block, share))
    attn_proj = jnp.concatenate(projections, axis=0)
    attn_proj = lax.dynamic_index_in_dim(attn_proj, my_half, 0, keepdims=False).astype(BF)
    moe = jnp.concatenate(moes, axis=1).reshape(tokens, share)
    moe = exchange(moe, GROUP + ("zhi",))
    moe = jnp.sum(moe.reshape(groups, halves, rows_here, share).astype(F32), axis=1).astype(BF)
    moe_out = moe.transpose(1, 0, 2).reshape(rows_here, width)
    return (attn_proj, moe_out)


def solution(mesh):
    fine = Mesh(mesh.devices.reshape(4, 2, 4, 4, 2), ("zlo", "core", "x", "y", "zhi"))
    g = GROUP
    e = XY + ("zhi",)
    in_specs = (
        P(g, e, None),
        P(g, e),
        P(g, None),
        P(g, None),
        P(g, None, None),
        P(g, None, None),
        P(g),
        P(e, None, None),
        P(e, None),
        P(g + e, None),
        P(),
        P(g + e, None),
        P(g + e, None),
        P(e, g, None),
        P(e, g, None),
        P(e, None, g),
    )
    out_specs = (P(g + e, None), P(g + e, None))
    return jax.shard_map(body, mesh=fine, in_specs=in_specs, out_specs=out_specs, check_vma=False)
```

```python
import functools

import jax
import jax.numpy as jnp
from jax import lax
from jax.experimental import pallas as pl
from jax.experimental.pallas import tpu as pltpu
from jax.sharding import Mesh, PartitionSpec as P

ROPE = 64
VD = 128
NORM_EPS = 1e-06
SCALE = (VD + ROPE) ** (-0.5)
RUNS = 4
CAP = 3
ROWS = 8
LINE_ORDER = (2, 1, 3)

SIDE = 4
LINES = 4
CORES = 2
HALVES = 2
GROUPS = LINES * CORES
PLANES = SIDE * SIDE
GROUP = ("zlo", "core")
XY = ("x", "y")
ALL = ("zlo", "core", "x", "y", "zhi")
SIZES = (LINES, CORES, SIDE, SIDE, HALVES)
BF = jnp.bfloat16
F32 = jnp.float32


def dot(a, b):
    return jnp.dot(a, b, preferred_element_type=F32)


def dot_t(a, b):
    return lax.dot_general(a, b, (((1,), (1,)), ((), ())), preferred_element_type=F32)


def dot_rows(a, b):
    return lax.dot_general(a, b, (((0,), (0,)), ((), ())), preferred_element_type=F32)


def split(value, count):
    pieces = []
    for _ in range(count):
        piece = lax.reduce_precision(value, 8, 7)
        pieces.append(piece.astype(BF))
        value = value - piece
    return pieces


def split_in_kernel(value):
    one = value.astype(BF)
    rest = value - one.astype(F32)
    two = rest.astype(BF)
    return one, two, (rest - two.astype(F32)).astype(BF)


def exchange(value, axes):
    return lax.all_to_all(value, axes, 0, 0, tiled=True)


def flips(count, k):
    return [(i, i ^ k) for i in range(count)]


def sum_wide(parts):
    total = parts[0].astype(F32)
    for part in parts[1:]:
        total = total + part.astype(F32)
    return total


def shift(k):
    return [(i, (i + k) % LINES) for i in range(LINES)]


def along_line(parts, sign=1):
    got = {k: lax.ppermute(parts[k], "zlo", shift(sign * k)) for k in LINE_ORDER}
    return [parts[0]] + [got[k] for k in range(1, LINES)]


def plane_shift(k, stage):
    pairs = []

    def number(place):
        flat = 0
        for size, one in zip(SIZES, place):
            flat = flat * size + one
        return flat

    for flat in range(LINES * CORES * PLANES * HALVES):
        place, rest = [], flat
        for size in reversed(SIZES):
            place.insert(0, rest % size)
            rest //= size
        there = list(place)
        axis = 2 if place[1] == stage else 3
        there[axis] = (there[axis] + k) % SIDE
        pairs.append((number(place), number(there)))
    return pairs


def one_hot(source, count):
    return (source[:, None] == jnp.arange(count, dtype=jnp.int32)[None, :]).astype(BF)


def plane_order(my_core):
    me = (lax.axis_index("x"), lax.axis_index("y"))
    row = jnp.arange(PLANES * HALVES * ROWS, dtype=jnp.int32)
    rest = row % (HALVES * ROWS)
    first = row // (HALVES * ROWS) // SIDE
    second = row // (HALVES * ROWS) % SIDE
    x = (me[0] + jnp.where(my_core == 0, first, second)) % SIDE
    y = (me[1] + jnp.where(my_core == 0, second, first)) % SIDE
    return one_hot((x * SIDE + y) * (HALVES * ROWS) + rest, row.shape[0])


def sorted_place(prompt_of_sample, my_line, my_core):
    samples = prompt_of_sample.shape[0]
    block = samples // (GROUPS * RUNS)
    own = prompt_of_sample.reshape(-1, block)[:, 0]
    at = jnp.arange(own.shape[0], dtype=jnp.int32)
    same = (own[:, None] == own[None, :]) & (at[None, :] < at[:, None])
    line = (own // CORES + LINES - my_line) % LINES
    seen = line * CORES + (own % CORES ^ my_core)
    rank = seen * RUNS + jnp.sum(same.astype(jnp.int32), axis=1)
    return jnp.repeat(rank, block) * block + jnp.arange(samples, dtype=jnp.int32) % block


def sort_kernel(q_latent_ref, q_rope_ref, place_ref, *out_refs):
    samples, heads, lat = q_latent_ref.shape
    order = place_ref[...] == lax.broadcasted_iota(jnp.int32, (samples, samples), 0)
    order = jnp.where(order, 1.0, 0.0).astype(BF)
    each = samples // LINES
    parts = [q_latent_ref[:, head, :] for head in range(heads)] + [q_rope_ref[...]]
    at = 0
    for part in parts:
        wide = dot(order, part).astype(BF)
        for k, out_ref in enumerate(out_refs):
            out_ref[:, at : at + part.shape[1]] = wide[k * each : (k + 1) * each]
        at += part.shape[1]


def attend_kernel(heads, *refs):
    q_refs, out_refs = refs[:LINES], refs[-LINES:]
    key_refs = refs[LINES : LINES + CORES]
    rope_refs = refs[LINES + CORES : LINES + 2 * CORES]
    w_uv_ref, table_ref = refs[LINES + 2 * CORES : LINES + 2 * CORES + 2]
    lat = key_refs[0].shape[1]
    each = q_refs[0].shape[0] // CORES
    rows = each * LINES
    column = lax.broadcasted_iota(jnp.int32, (rows, VD), 1)
    for core in range(CORES):
        mine = slice(core * each, (core + 1) * each)
        q = jnp.concatenate([ref[mine, :] for ref in q_refs], axis=0)
        keys = key_refs[core][...]
        rope_keys = rope_refs[core][...]
        none = jnp.zeros_like(rope_keys)
        extra = jnp.concatenate([table_ref[mine, :]] * LINES, axis=0).astype(F32)
        for head in range(heads):
            pair = [rope_keys if head == one else none for one in range(heads)]
            score = dot_t(q[:, head * lat : (head + 1) * lat], keys)
            score = (score + dot(q[:, heads * lat :], jnp.concatenate(pair, axis=0))) * SCALE
            best = jnp.max(score, axis=-1, keepdims=True)
            weight = jnp.exp(score - best)
            total = jnp.sum(weight, axis=-1, keepdims=True)
            latent = (dot(weight.astype(BF), keys) / total).astype(BF)
            value = dot(latent, w_uv_ref[head]).astype(BF)
            for k, out_ref in enumerate(out_refs):
                out_ref[mine, head * VD : (head + 1) * VD] = value[k * each : (k + 1) * each]
            for place, piece in enumerate(split_in_kernel(best + jnp.log(total))):
                extra = jnp.where(column == 3 * head + place, piece.astype(F32), extra)
        extra = extra.astype(BF)
        for k, out_ref in enumerate(out_refs):
            out_ref[mine, heads * VD :] = extra[k * each : (k + 1) * each]


def merge_kernel(heads, *refs):
    back_refs = refs[:LINES]
    place_ref, order_ref, self_score_ref, self_latent_ref, w_uv_ref, out_ref = refs[LINES:]
    back = jnp.concatenate([ref[...] for ref in back_refs], axis=0)
    samples = back.shape[0]
    to_place = place_ref[...] == lax.broadcasted_iota(jnp.int32, (samples, samples), 0)
    back = dot_rows(jnp.where(to_place, 1.0, 0.0).astype(BF), back)
    values = []
    for head in range(heads):
        at = heads * VD + 3 * head
        lse = back[:, at : at + 1] + back[:, at + 1 : at + 2] + back[:, at + 2 : at + 3]
        self_score = self_score_ref[:, head : head + 1]
        best = jnp.maximum(lse, self_score)
        cache_part = jnp.exp(lse - best)
        self_part = jnp.exp(self_score - best)
        own_value = dot(self_latent_ref[...], w_uv_ref[head])
        mixed = cache_part * back[:, head * VD : (head + 1) * VD] + self_part * own_value
        values.append((mixed / (cache_part + self_part)).astype(BF))
    out_ref[...] = dot(order_ref[...], jnp.concatenate(values, axis=1)).astype(BF)


def up_kernel(line_ref, rows_ref, *refs):
    w_refs, out_refs = refs[: 2 * CORES], refs[2 * CORES :]
    each = rows_ref.shape[0] // LINES
    share = rows_ref.shape[1] // CORES
    line = line_ref[0]
    rows = []
    for k in range(LINES):
        at = pl.multiple_of(lax.rem(line + k, LINES) * each, each)
        rows.append(rows_ref[pl.ds(at, each), :])
    rows = jnp.concatenate(rows, axis=0)
    for half in range(2):
        total = dot(rows[:, :share], w_refs[half][...]) + dot(rows[:, share:], w_refs[2 + half][...])
        total = total.astype(BF)
        width = total.shape[1]
        for k, out_ref in enumerate(out_refs):
            out_ref[:, half * width : (half + 1) * width] = total[k * each : (k + 1) * each]


def down_kernel(line_ref, *refs):
    hidden_refs, w_refs, out_ref = refs[:LINES], refs[LINES : LINES + CORES], refs[-1]
    each = hidden_refs[0].shape[0]
    line = line_ref[0]
    hidden = jnp.concatenate([ref[...] for ref in hidden_refs], axis=0)
    for core in range(CORES):
        total = dot(hidden, w_refs[core][...]).astype(BF)
        width = total.shape[1]
        for k in range(LINES):
            at = pl.multiple_of(lax.rem(line + LINES - k, LINES) * each, each)
            out_ref[pl.ds(at, each), core * width : (core + 1) * width] = total[k * each : (k + 1) * each]


def on_chip(kernel, shapes, *args):
    vmem = pl.BlockSpec(memory_space=pltpu.VMEM)
    smem = pl.BlockSpec(memory_space=pltpu.SMEM)
    return pl.pallas_call(
        kernel,
        out_shape=[jax.ShapeDtypeStruct(shape, BF) for shape in shapes],
        in_specs=[smem if one.shape == (1,) else vmem for one in args],
        out_specs=[vmem] * len(shapes),
        compiler_params=pltpu.CompilerParams(vmem_limit_bytes=48 * 1024 * 1024),
    )(*args)


def routing_tables(ids, gates, my_half, order):
    tokens = ids.shape[0]
    slots = tokens // ROWS * CAP
    wanted = jnp.arange(PLANES, dtype=jnp.int32) * HALVES + my_half
    hit = ids[:, :, None] == wanted[None, None, :]
    member = jnp.any(hit, axis=1)
    gate_of = jnp.sum(jnp.where(hit, gates[:, :, None], 0.0), axis=1)
    before = jnp.cumsum(member.astype(jnp.int32), axis=0) - member.astype(jnp.int32)
    place = jnp.where(member, before, -1).T
    routed = place[:, None, :] == jnp.arange(slots, dtype=jnp.int32)[None, :, None]
    routed = routed.reshape(PLANES * slots, tokens)
    weights = jnp.where(routed, jnp.repeat(gate_of.T, slots, axis=0), 0.0)
    routing = jnp.take(routed.astype(BF).reshape(PLANES * slots, LINES, -1), order, axis=1)
    return (routing.reshape(PLANES * slots, tokens), *split(weights, 2))


def body(
    q_latent,
    q_rope,
    self_latent,
    self_rope,
    cache_latent,
    cache_rope,
    prompt_of_sample,
    w_uv,
    w_out,
    residual,
    norm_gain,
    expert_ids,
    gate_weight,
    w_gate,
    w_up,
    w_down,
):
    my_half = lax.axis_index("zhi")
    my_core = lax.axis_index("core")
    my_line = lax.axis_index("zlo")
    line = my_line.astype(jnp.int32).reshape(1)
    lines = jnp.arange(LINES, dtype=jnp.int32)
    samples, heads, lat = q_latent.shape
    width = residual.shape[1]
    share = width // GROUPS
    top = expert_ids.shape[1]
    tokens = LINES * HALVES * ROWS
    each = samples // LINES

    def sibling(value):
        return lax.ppermute(value, "core", flips(CORES, 1))

    place = sorted_place(prompt_of_sample, my_line, my_core)[None, :]
    q_sorted = on_chip(
        sort_kernel, [(each, heads * lat + heads * ROPE)] * LINES, q_latent, q_rope, place
    )
    q_here = along_line(q_sorted)
    keys = [cache_latent[0], sibling(cache_latent[0])]
    rope_keys = [cache_rope[0], sibling(cache_rope[0])]

    own_table = jnp.concatenate([expert_ids.astype(BF), *split(gate_weight, 3)], axis=1)
    other_table = lax.ppermute(own_table, "zhi", flips(HALVES, 1))
    table = jnp.concatenate(
        [
            jnp.where(my_half == 0, own_table, other_table),
            jnp.where(my_half == 0, other_table, own_table),
        ],
        axis=0,
    )
    stats = 3 * heads
    table_pad = jnp.pad(
        table, ((0, each - table.shape[0]), (stats, VD - stats - table.shape[1]))
    )
    back = on_chip(
        functools.partial(attend_kernel, heads),
        [(each, (heads + 1) * VD)] * LINES,
        *q_here,
        *keys,
        *rope_keys,
        w_uv,
        table_pad,
    )
    back = along_line(back, -1)
    self_wide = self_latent.astype(F32)
    self_pos = self_rope.astype(F32)
    self_score = [
        jnp.sum(q_latent[:, head].astype(F32) * self_wide, axis=-1)
        + jnp.sum(q_rope[:, head * ROPE : (head + 1) * ROPE].astype(F32) * self_pos, axis=-1)
        for head in range(heads)
    ]
    self_score = jnp.stack(self_score, axis=1) * SCALE
    (head_rows,) = on_chip(
        functools.partial(merge_kernel, heads),
        [(samples, heads * VD)],
        *back,
        place,
        plane_order(my_core),
        self_score,
        self_latent,
        w_uv,
    )

    rows = head_rows.reshape(SIDE, samples // SIDE, -1)
    first = [dot(rows[k], w_out).astype(BF) for k in range(SIDE)]
    first = sum_wide([first[0]] + [lax.ppermute(first[k], ALL, plane_shift(k, 0)) for k in (2, 1, 3)])
    first = first.astype(BF).reshape(SIDE, HALVES * ROWS, width)
    near = sum_wide([first[0]] + [lax.ppermute(first[k], ALL, plane_shift(k, 1)) for k in (2, 1, 3)])

    near = near.reshape(HALVES, ROWS, width)
    is_mine = (jnp.arange(HALVES) == my_half)[:, None, None]
    with_residual = near + jnp.where(is_mine, residual.astype(F32)[None], 0.0)
    far = lax.ppermute(with_residual.astype(BF), "zhi", flips(HALVES, 1)).astype(F32)
    attn_proj = lax.dynamic_index_in_dim(near + far, my_half, 0, keepdims=False).astype(BF)
    mixed = with_residual + far
    normed = (
        mixed * lax.rsqrt(jnp.mean(mixed * mixed, axis=-1, keepdims=True) + NORM_EPS) * norm_gain
    ).astype(BF)

    by_chip = normed.reshape(HALVES * ROWS, LINES, CORES, share)
    by_chip = jnp.where(my_core == 0, by_chip, by_chip[:, :, ::-1]).reshape(-1, LINES, CORES * share)
    by_chip = jnp.take(by_chip.transpose(1, 0, 2), (my_line + LINES - lines) % LINES, axis=0)
    token_rows = jnp.concatenate(along_line([by_chip[k] for k in range(LINES)], -1), axis=0)

    table = jnp.stack([one[: HALVES * ROWS, heads * VD + stats :] for one in back])
    table = jnp.take(table, (lines + LINES - my_line) % LINES, axis=0)
    table = table.reshape(tokens, -1).astype(F32)
    gates = table[:, top : 2 * top] + table[:, 2 * top : 3 * top] + table[:, 3 * top : 4 * top]
    routing, gate_hi, gate_lo = routing_tables(
        table[:, :top].astype(jnp.int32), gates, my_half, (lines + my_line) % LINES
    )
    rows_in = exchange(dot(routing, token_rows).astype(BF), XY)

    line_rows = rows_in.shape[0] // LINES
    parts = on_chip(
        up_kernel,
        [(line_rows, 2 * w_gate.shape[2])] * LINES,
        line,
        rows_in,
        w_gate[0],
        w_up[0],
        sibling(w_gate[0]),
        sibling(w_up[0]),
    )
    sums = sum_wide(along_line(parts))
    ffe = sums.shape[1] // 2
    hidden = (jax.nn.silu(sums[:, :ffe]) * sums[:, ffe:]).astype(BF)
    (expert_out,) = on_chip(
        down_kernel,
        [(rows_in.shape[0], CORES * share)],
        line,
        *along_line([hidden] * LINES),
        w_down[0],
        sibling(w_down[0]),
    )

    returned = exchange(expert_out, XY)
    moe = dot_rows(gate_hi, returned) + dot_rows(gate_lo, returned)
    moe = exchange(moe.astype(BF), ("zlo", "zhi"))
    moe = jnp.sum(moe.reshape(LINES, HALVES, ROWS, CORES, share).astype(F32), axis=1).astype(BF)
    moe = jnp.where(my_core == 0, moe, moe[:, :, ::-1])
    moe_out = moe.transpose(1, 0, 2, 3).reshape(ROWS, width)
    return (attn_proj, moe_out)


def solution(mesh):
    fine = Mesh(mesh.devices.reshape(SIZES), ALL)
    g = GROUP
    e = XY + ("zhi",)
    in_specs = (
        P(g, e, None),
        P(g, e),
        P(g, None),
        P(g, None),
        P(g, None, None),
        P(g, None, None),
        P(g),
        P(e, None, None),
        P(e, None),
        P(g + e, None),
        P(),
        P(g + e, None),
        P(g + e, None),
        P(e, g, None),
        P(e, g, None),
        P(e, None, g),
    )
    out_specs = (P(g + e, None), P(g + e, None))
    return jax.shard_map(body, mesh=fine, in_specs=in_specs, out_specs=out_specs, check_vma=False)
```

```python
import functools

import jax
import jax.numpy as jnp
from jax import lax
from jax.experimental import pallas as pl
from jax.experimental.pallas import tpu as pltpu
from jax.sharding import Mesh, PartitionSpec as P

ROPE = 64
VD = 128
NORM_EPS = 1e-06
SCALE = (VD + ROPE) ** (-0.5)
RUNS = 4
CAP = 3
ROWS = 8
LINE_ORDER = (2, 1, 3)
UP_STEPS = 4

SIDE = 4
LINES = 4
CORES = 2
HALVES = 2
GROUPS = LINES * CORES
PLANES = SIDE * SIDE
GROUP = ("zlo", "core")
XY = ("x", "y")
ALL = ("zlo", "core", "x", "y", "zhi")
SIZES = (LINES, CORES, SIDE, SIDE, HALVES)
BF = jnp.bfloat16
F32 = jnp.float32


def dot(a, b):
    return jnp.dot(a, b, preferred_element_type=F32)


def dot_t(a, b):
    return lax.dot_general(a, b, (((1,), (1,)), ((), ())), preferred_element_type=F32)


def dot_rows(a, b):
    return lax.dot_general(a, b, (((0,), (0,)), ((), ())), preferred_element_type=F32)


def split(value, count):
    pieces = []
    for _ in range(count):
        piece = lax.reduce_precision(value, 8, 7)
        pieces.append(piece.astype(BF))
        value = value - piece
    return pieces


def split_in_kernel(value):
    one = value.astype(BF)
    rest = value - one.astype(F32)
    two = rest.astype(BF)
    return one, two, (rest - two.astype(F32)).astype(BF)


def exchange(value, axes):
    return lax.all_to_all(value, axes, 0, 0, tiled=True)


def flips(count, k):
    return [(i, i ^ k) for i in range(count)]


def sum_wide(parts):
    total = parts[0].astype(F32)
    for part in parts[1:]:
        total = total + part.astype(F32)
    return total


def shift(k):
    return [(i, (i + k) % LINES) for i in range(LINES)]


def along_line(parts, sign=1):
    got = {k: lax.ppermute(parts[k], "zlo", shift(sign * k)) for k in LINE_ORDER}
    return [parts[0]] + [got[k] for k in range(1, LINES)]


def plane_shift(k, stage):
    pairs = []

    def number(place):
        flat = 0
        for size, one in zip(SIZES, place):
            flat = flat * size + one
        return flat

    for flat in range(LINES * CORES * PLANES * HALVES):
        place, rest = [], flat
        for size in reversed(SIZES):
            place.insert(0, rest % size)
            rest //= size
        there = list(place)
        axis = 2 if place[1] == stage else 3
        there[axis] = (there[axis] + k) % SIDE
        pairs.append((number(place), number(there)))
    return pairs


def one_hot(source, count):
    return (source[:, None] == jnp.arange(count, dtype=jnp.int32)[None, :]).astype(BF)


def plane_order(my_core):
    me = (lax.axis_index("x"), lax.axis_index("y"))
    row = jnp.arange(PLANES * HALVES * ROWS, dtype=jnp.int32)
    rest = row % (HALVES * ROWS)
    first = row // (HALVES * ROWS) // SIDE
    second = row // (HALVES * ROWS) % SIDE
    x = (me[0] + jnp.where(my_core == 0, first, second)) % SIDE
    y = (me[1] + jnp.where(my_core == 0, second, first)) % SIDE
    return one_hot((x * SIDE + y) * (HALVES * ROWS) + rest, row.shape[0])


def sorted_place(prompt_of_sample, my_line, my_core):
    samples = prompt_of_sample.shape[0]
    block = samples // (GROUPS * RUNS)
    own = prompt_of_sample.reshape(-1, block)[:, 0]
    at = jnp.arange(own.shape[0], dtype=jnp.int32)
    same = (own[:, None] == own[None, :]) & (at[None, :] < at[:, None])
    line = (own // CORES + LINES - my_line) % LINES
    seen = line * CORES + (own % CORES ^ my_core)
    rank = seen * RUNS + jnp.sum(same.astype(jnp.int32), axis=1)
    return jnp.repeat(rank, block) * block + jnp.arange(samples, dtype=jnp.int32) % block


def sort_kernel(q_latent_ref, q_rope_ref, place_ref, *out_refs):
    samples, heads, lat = q_latent_ref.shape
    order = place_ref[...] == lax.broadcasted_iota(jnp.int32, (samples, samples), 0)
    order = jnp.where(order, 1.0, 0.0).astype(BF)
    each = samples // LINES
    parts = [q_latent_ref[:, head, :] for head in range(heads)] + [q_rope_ref[...]]
    at = 0
    for part in parts:
        wide = dot(order, part).astype(BF)
        for k, out_ref in enumerate(out_refs):
            out_ref[:, at : at + part.shape[1]] = wide[k * each : (k + 1) * each]
        at += part.shape[1]


def attend_kernel(heads, *refs):
    q_refs, out_refs = refs[:LINES], refs[-LINES:]
    key_refs = refs[LINES : LINES + CORES]
    rope_refs = refs[LINES + CORES : LINES + 2 * CORES]
    w_uv_ref, table_ref = refs[LINES + 2 * CORES : LINES + 2 * CORES + 2]
    lat = key_refs[0].shape[1]
    each = q_refs[0].shape[0] // CORES
    rows = each * LINES
    column = lax.broadcasted_iota(jnp.int32, (rows, VD), 1)
    for core in range(CORES):
        mine = slice(core * each, (core + 1) * each)
        q = jnp.concatenate([ref[mine, :] for ref in q_refs], axis=0)
        keys = key_refs[core][...]
        rope_keys = rope_refs[core][...]
        none = jnp.zeros_like(rope_keys)
        extra = jnp.concatenate([table_ref[mine, :]] * LINES, axis=0).astype(F32)
        for head in range(heads):
            pair = [rope_keys if head == one else none for one in range(heads)]
            score = dot_t(q[:, head * lat : (head + 1) * lat], keys)
            score = (score + dot(q[:, heads * lat :], jnp.concatenate(pair, axis=0))) * SCALE
            best = jnp.max(score, axis=-1, keepdims=True)
            weight = jnp.exp(score - best)
            total = jnp.sum(weight, axis=-1, keepdims=True)
            latent = (dot(weight.astype(BF), keys) / total).astype(BF)
            value = dot(latent, w_uv_ref[head]).astype(BF)
            for k, out_ref in enumerate(out_refs):
                out_ref[mine, head * VD : (head + 1) * VD] = value[k * each : (k + 1) * each]
            for place, piece in enumerate(split_in_kernel(best + jnp.log(total))):
                extra = jnp.where(column == 3 * head + place, piece.astype(F32), extra)
        extra = extra.astype(BF)
        for k, out_ref in enumerate(out_refs):
            out_ref[mine, heads * VD :] = extra[k * each : (k + 1) * each]


def merge_kernel(heads, *refs):
    back_refs = refs[:LINES]
    place_ref, order_ref, self_score_ref, self_latent_ref, w_uv_ref, w_out_ref = refs[LINES:-SIDE]
    out_refs = refs[-SIDE:]
    back = jnp.concatenate([ref[...] for ref in back_refs], axis=0)
    samples = back.shape[0]
    to_place = place_ref[...] == lax.broadcasted_iota(jnp.int32, (samples, samples), 0)
    back = dot_rows(jnp.where(to_place, 1.0, 0.0).astype(BF), back)
    values = []
    for head in range(heads):
        at = heads * VD + 3 * head
        lse = back[:, at : at + 1] + back[:, at + 1 : at + 2] + back[:, at + 2 : at + 3]
        self_score = self_score_ref[:, head : head + 1]
        best = jnp.maximum(lse, self_score)
        cache_part = jnp.exp(lse - best)
        self_part = jnp.exp(self_score - best)
        own_value = dot(self_latent_ref[...], w_uv_ref[head])
        mixed = cache_part * back[:, head * VD : (head + 1) * VD] + self_part * own_value
        values.append((mixed / (cache_part + self_part)).astype(BF))
    rows = dot(order_ref[...], jnp.concatenate(values, axis=1)).astype(BF)
    width = w_out_ref.shape[1] // LINES
    for part in range(LINES):
        columns = slice(part * width, (part + 1) * width)
        total = dot(rows, w_out_ref[:, columns]).astype(BF)
        for k, out_ref in enumerate(out_refs):
            each = out_ref.shape[0]
            out_ref[:, columns] = total[k * each : (k + 1) * each]


def own_rows(half, rows):
    return jnp.where(half == 0, rows[:ROWS], rows[ROWS:])


def with_own(half, rows, residual):
    first = jnp.where(half == 0, residual, 0.0)
    return rows + jnp.concatenate([first, residual - first], axis=0)


def near_kernel(half_ref, *refs):
    part_refs, residual_ref, near_ref, out_ref = refs[:SIDE], refs[SIDE], refs[-2], refs[-1]
    near = sum_wide([ref[...] for ref in part_refs])
    near_ref[...] = near
    out_ref[...] = with_own(half_ref[0], near, residual_ref[...].astype(F32)).astype(BF)


def norm_kernel(half_ref, line_ref, core_ref, near_ref, far_ref, residual_ref, gain_ref, *refs):
    attn_ref, out_refs, scratch = refs[0], refs[1:-1], refs[-1]
    half, line, core = half_ref[0], line_ref[0], core_ref[0]
    total = near_ref[...] + far_ref[...].astype(F32)
    attn_ref[...] = own_rows(half, total).astype(BF)
    mixed = with_own(half, total, residual_ref[...].astype(F32))
    scale = lax.rsqrt(jnp.mean(mixed * mixed, axis=-1, keepdims=True) + NORM_EPS)
    scratch[...] = (mixed * scale * gain_ref[...]).astype(BF)
    share = scratch.shape[1] // GROUPS
    for k, out_ref in enumerate(out_refs):
        chip = lax.rem(line + LINES - k, LINES) * CORES
        for side in range(CORES):
            at = pl.multiple_of((chip + (core + side) % CORES) * share, share)
            out_ref[:, side * share : (side + 1) * share] = scratch[:, pl.ds(at, share)]


def up_kernel(line_ref, rows_ref, *refs):
    w_refs, out_refs, rows_scratch = refs[: 2 * CORES], refs[2 * CORES : -1], refs[-1]
    each = rows_ref.shape[0] // LINES
    share = rows_ref.shape[1] // CORES
    step = pl.program_id(0)

    @pl.when(step == 0)
    def _():
        line = line_ref[0]
        for k in range(LINES):
            at = pl.multiple_of(lax.rem(line + k, LINES) * each, each)
            rows_scratch[k * each : (k + 1) * each, :] = rows_ref[pl.ds(at, each), :]

    rows = rows_scratch[...]
    for half in range(2):
        total = dot(rows[:, :share], w_refs[half][...]) + dot(rows[:, share:], w_refs[2 + half][...])
        total = total.astype(BF)
        width = total.shape[1]
        at = pl.multiple_of((half * pl.num_programs(0) + step) * width, width)
        for k, out_ref in enumerate(out_refs):
            out_ref[:, pl.ds(at, width)] = total[k * each : (k + 1) * each]


def down_kernel(line_ref, *refs):
    hidden_refs, w_refs, out_ref, total_ref = refs[:LINES], refs[LINES : LINES + CORES], refs[-2], refs[-1]
    each = hidden_refs[0].shape[0]
    step = pl.program_id(0)
    depth = w_refs[0].shape[0]
    width = w_refs[0].shape[1]
    at = pl.multiple_of(step * depth, depth)
    hidden = jnp.concatenate([ref[:, pl.ds(at, depth)] for ref in hidden_refs], axis=0)
    for core in range(CORES):
        columns = slice(core * width, (core + 1) * width)
        total = dot(hidden, w_refs[core][...])

        @pl.when(step == 0)
        def _():
            total_ref[:, columns] = total

        @pl.when(step == pl.num_programs(0) - 1)
        def _():
            line = line_ref[0]
            whole = (total_ref[:, columns] + total).astype(BF)
            for k in range(LINES):
                at = pl.multiple_of(lax.rem(line + LINES - k, LINES) * each, each)
                out_ref[pl.ds(at, each), columns] = whole[k * each : (k + 1) * each]


def whole(shape):
    return pl.BlockSpec(shape, lambda step: (0, 0))


def column_block(one, count):
    return pl.BlockSpec((one.shape[0], one.shape[1] // count), lambda step: (0, step))


def row_block(one, count):
    return pl.BlockSpec((one.shape[0] // count, one.shape[1]), lambda step: (step, 0))


def on_chip(kernel, shapes, *args, dtypes=None, **more):
    vmem = pl.BlockSpec(memory_space=pltpu.VMEM)
    smem = pl.BlockSpec(memory_space=pltpu.SMEM)
    more.setdefault("in_specs", [smem if one.shape == (1,) else vmem for one in args])
    more.setdefault("out_specs", [vmem] * len(shapes))
    return pl.pallas_call(
        kernel,
        out_shape=[
            jax.ShapeDtypeStruct(shape, dtype)
            for shape, dtype in zip(shapes, dtypes or [BF] * len(shapes))
        ],
        compiler_params=pltpu.CompilerParams(vmem_limit_bytes=48 * 1024 * 1024),
        **more,
    )(*args)


def routing_tables(ids, gates, my_half, order):
    tokens = ids.shape[0]
    slots = tokens // ROWS * CAP
    wanted = jnp.arange(PLANES, dtype=jnp.int32) * HALVES + my_half
    hit = ids[:, :, None] == wanted[None, None, :]
    member = jnp.any(hit, axis=1)
    gate_of = jnp.sum(jnp.where(hit, gates[:, :, None], 0.0), axis=1)
    before = jnp.cumsum(member.astype(jnp.int32), axis=0) - member.astype(jnp.int32)
    place = jnp.where(member, before, -1).T
    routed = place[:, None, :] == jnp.arange(slots, dtype=jnp.int32)[None, :, None]
    routed = routed.reshape(PLANES * slots, tokens)
    weights = jnp.where(routed, jnp.repeat(gate_of.T, slots, axis=0), 0.0)
    routing = jnp.take(routed.astype(BF).reshape(PLANES * slots, LINES, -1), order, axis=1)
    return (routing.reshape(PLANES * slots, tokens), *split(weights, 2))


def body(
    q_latent,
    q_rope,
    self_latent,
    self_rope,
    cache_latent,
    cache_rope,
    prompt_of_sample,
    w_uv,
    w_out,
    residual,
    norm_gain,
    expert_ids,
    gate_weight,
    w_gate,
    w_up,
    w_down,
):
    my_half = lax.axis_index("zhi")
    my_core = lax.axis_index("core")
    my_line = lax.axis_index("zlo")
    line = my_line.astype(jnp.int32).reshape(1)
    lines = jnp.arange(LINES, dtype=jnp.int32)
    samples, heads, lat = q_latent.shape
    width = residual.shape[1]
    share = width // GROUPS
    top = expert_ids.shape[1]
    tokens = LINES * HALVES * ROWS
    each = samples // LINES

    def sibling(value):
        return lax.ppermute(value, "core", flips(CORES, 1))

    place = sorted_place(prompt_of_sample, my_line, my_core)[None, :]
    q_sorted = on_chip(
        sort_kernel, [(each, heads * lat + heads * ROPE)] * LINES, q_latent, q_rope, place
    )
    q_here = along_line(q_sorted)
    keys = [cache_latent[0], sibling(cache_latent[0])]
    rope_keys = [cache_rope[0], sibling(cache_rope[0])]

    table = jnp.concatenate([expert_ids.astype(BF), *split(gate_weight, 3)], axis=1)
    stats = 3 * heads
    table_pad = jnp.pad(
        table, ((0, each - table.shape[0]), (stats, VD - stats - table.shape[1]))
    )
    back = on_chip(
        functools.partial(attend_kernel, heads),
        [(each, (heads + 1) * VD)] * LINES,
        *q_here,
        *keys,
        *rope_keys,
        w_uv,
        table_pad,
    )
    back = along_line(back, -1)
    self_wide = self_latent.astype(F32)
    self_pos = self_rope.astype(F32)
    self_score = [
        jnp.sum(q_latent[:, head].astype(F32) * self_wide, axis=-1)
        + jnp.sum(q_rope[:, head * ROPE : (head + 1) * ROPE].astype(F32) * self_pos, axis=-1)
        for head in range(heads)
    ]
    self_score = jnp.stack(self_score, axis=1) * SCALE
    first = on_chip(
        functools.partial(merge_kernel, heads),
        [(samples // SIDE, width)] * SIDE,
        *back,
        place,
        plane_order(my_core),
        self_score,
        self_latent,
        w_uv,
        w_out,
    )
    first = sum_wide([first[0]] + [lax.ppermute(first[k], ALL, plane_shift(k, 0)) for k in (2, 1, 3)])
    first = first.astype(BF).reshape(SIDE, HALVES * ROWS, width)
    second = [first[0]] + [lax.ppermute(first[k], ALL, plane_shift(k, 1)) for k in (1, 2, 3)]
    half = my_half.astype(jnp.int32).reshape(1)
    near, outgoing = on_chip(
        near_kernel,
        [(HALVES * ROWS, width)] * 2,
        half,
        *second,
        residual,
        dtypes=[F32, BF],
    )
    far = lax.ppermute(outgoing, "zhi", flips(HALVES, 1))
    attn_proj, *by_chip = on_chip(
        norm_kernel,
        [(ROWS, width)] + [(HALVES * ROWS, CORES * share)] * LINES,
        half,
        line,
        my_core.astype(jnp.int32).reshape(1),
        near,
        far,
        residual,
        norm_gain.reshape(1, -1),
        scratch_shapes=[pltpu.VMEM((HALVES * ROWS, width), BF)],
    )

    token_rows = jnp.concatenate(along_line(by_chip, -1), axis=0)

    table = jnp.stack([one[:ROWS, heads * VD + stats : heads * VD + stats + 4 * top] for one in back])
    other = lax.ppermute(table, "zhi", flips(HALVES, 1))
    pair = [jnp.where(my_half == 0, table, other), jnp.where(my_half == 0, other, table)]
    table = jnp.concatenate(pair, axis=1)
    table = jnp.take(table, (lines + LINES - my_line) % LINES, axis=0)
    table = table.reshape(tokens, -1).astype(F32)
    gates = table[:, top : 2 * top] + table[:, 2 * top : 3 * top] + table[:, 3 * top : 4 * top]
    routing, gate_hi, gate_lo = routing_tables(
        table[:, :top].astype(jnp.int32), gates, my_half, (lines + my_line) % LINES
    )
    rows_in = exchange(dot(routing, token_rows).astype(BF), XY)

    line_rows = rows_in.shape[0] // LINES
    ups = [w_gate[0], w_up[0], sibling(w_gate[0]), sibling(w_up[0])]
    scalar = pl.BlockSpec(memory_space=pltpu.SMEM)
    out_shape = (line_rows, 2 * w_gate.shape[2])
    parts = on_chip(
        up_kernel,
        [out_shape] * LINES,
        line,
        rows_in,
        *ups,
        grid=(UP_STEPS,),
        in_specs=[scalar, whole(rows_in.shape)] + [column_block(one, UP_STEPS) for one in ups],
        out_specs=[whole(out_shape)] * LINES,
        scratch_shapes=[pltpu.VMEM(rows_in.shape, BF)],
    )
    sums = sum_wide(along_line(parts))
    ffe = sums.shape[1] // 2
    hidden = (jax.nn.silu(sums[:, :ffe]) * sums[:, ffe:]).astype(BF)
    downs = [w_down[0], sibling(w_down[0])]
    out_shape = (rows_in.shape[0], CORES * share)
    (expert_out,) = on_chip(
        down_kernel,
        [out_shape],
        line,
        *along_line([hidden] * LINES),
        *downs,
        grid=(2,),
        in_specs=[scalar] + [whole(hidden.shape)] * LINES + [row_block(one, 2) for one in downs],
        out_specs=[whole(out_shape)],
        scratch_shapes=[pltpu.VMEM(out_shape, F32)],
    )

    returned = exchange(expert_out, XY)
    moe = dot_rows(gate_hi, returned) + dot_rows(gate_lo, returned)
    moe = exchange(moe.astype(BF), ("zlo", "zhi"))
    moe = jnp.sum(moe.reshape(LINES, HALVES, ROWS, CORES, share).astype(F32), axis=1).astype(BF)
    moe = jnp.where(my_core == 0, moe, moe[:, :, ::-1])
    moe_out = moe.transpose(1, 0, 2, 3).reshape(ROWS, width)
    return (attn_proj, moe_out)


def solution(mesh):
    fine = Mesh(mesh.devices.reshape(SIZES), ALL)
    g = GROUP
    e = XY + ("zhi",)
    in_specs = (
        P(g, e, None),
        P(g, e),
        P(g, None),
        P(g, None),
        P(g, None, None),
        P(g, None, None),
        P(g),
        P(e, None, None),
        P(e, None),
        P(g + e, None),
        P(),
        P(g + e, None),
        P(g + e, None),
        P(e, g, None),
        P(e, g, None),
        P(e, None, g),
    )
    out_specs = (P(g + e, None), P(g + e, None))
    return jax.shard_map(body, mesh=fine, in_specs=in_specs, out_specs=out_specs, check_vma=False)
```

```python
import functools

import jax
import jax.numpy as jnp
from jax import lax
from jax.experimental import pallas as pl
from jax.experimental.pallas import tpu as pltpu
from jax.sharding import Mesh, PartitionSpec as P

ROPE = 64
VD = 128
NORM_EPS = 1e-06
SCALE = (VD + ROPE) ** (-0.5)
RUNS = 4
CAP = 3
ROWS = 8
LINE_ORDER = (2, 1, 3)
UP_STEPS = 4
FLIP_ORDER = (0, 2, 1, 3)

SIDE = 4
LINES = 4
CORES = 2
HALVES = 2
GROUPS = LINES * CORES
PLANES = SIDE * SIDE
GROUP = ("zlo", "core")
XY = ("x", "y")
ALL = ("zlo", "core", "x", "y", "zhi")
SIZES = (LINES, CORES, SIDE, SIDE, HALVES)
BF = jnp.bfloat16
F32 = jnp.float32


def dot(a, b):
    return jnp.dot(a, b, preferred_element_type=F32)


def dot_t(a, b):
    return lax.dot_general(a, b, (((1,), (1,)), ((), ())), preferred_element_type=F32)


def dot_rows(a, b):
    return lax.dot_general(a, b, (((0,), (0,)), ((), ())), preferred_element_type=F32)


def split(value, count):
    pieces = []
    for _ in range(count):
        piece = lax.reduce_precision(value, 8, 7)
        pieces.append(piece.astype(BF))
        value = value - piece
    return pieces


def split_in_kernel(value):
    one = value.astype(BF)
    rest = value - one.astype(F32)
    two = rest.astype(BF)
    return one, two, (rest - two.astype(F32)).astype(BF)


def exchange(value, axes):
    return lax.all_to_all(value, axes, 0, 0, tiled=True)


def flips(count, k):
    return [(i, i ^ k) for i in range(count)]


def sum_wide(parts):
    total = parts[0].astype(F32)
    for part in parts[1:]:
        total = total + part.astype(F32)
    return total


def shift(k):
    return [(i, (i + k) % LINES) for i in range(LINES)]


def along_line(parts, sign=1):
    got = {k: lax.ppermute(parts[k], "zlo", shift(sign * k)) for k in LINE_ORDER}
    return [parts[0]] + [got[k] for k in range(1, LINES)]


def plane_shift(k, stage):
    pairs = []

    def number(place):
        flat = 0
        for size, one in zip(SIZES, place):
            flat = flat * size + one
        return flat

    for flat in range(LINES * CORES * PLANES * HALVES):
        place, rest = [], flat
        for size in reversed(SIZES):
            place.insert(0, rest % size)
            rest //= size
        there = list(place)
        axis = 2 if place[1] == stage else 3
        there[axis] = (there[axis] + k) % SIDE
        pairs.append((number(place), number(there)))
    return pairs


def one_hot(source, count):
    return (source[:, None] == jnp.arange(count, dtype=jnp.int32)[None, :]).astype(BF)


def plane_order(my_core):
    me = (lax.axis_index("x"), lax.axis_index("y"))
    row = jnp.arange(PLANES * HALVES * ROWS, dtype=jnp.int32)
    rest = row % (HALVES * ROWS)
    first = row // (HALVES * ROWS) // SIDE
    second = row // (HALVES * ROWS) % SIDE
    x = (me[0] + jnp.where(my_core == 0, first, second)) % SIDE
    y = (me[1] + jnp.where(my_core == 0, second, first)) % SIDE
    return one_hot((x * SIDE + y) * (HALVES * ROWS) + rest, row.shape[0])


def sorted_place(prompt_of_sample, my_line, my_core):
    samples = prompt_of_sample.shape[0]
    block = samples // (GROUPS * RUNS)
    own = prompt_of_sample.reshape(-1, block)[:, 0]
    at = jnp.arange(own.shape[0], dtype=jnp.int32)
    same = (own[:, None] == own[None, :]) & (at[None, :] < at[:, None])
    line = (own // CORES + LINES - my_line) % LINES
    seen = line * CORES + (own % CORES ^ my_core)
    rank = seen * RUNS + jnp.sum(same.astype(jnp.int32), axis=1)
    return jnp.repeat(rank, block) * block + jnp.arange(samples, dtype=jnp.int32) % block


def sort_kernel(q_latent_ref, q_rope_ref, place_ref, *out_refs):
    samples, heads, lat = q_latent_ref.shape
    order = place_ref[...] == lax.broadcasted_iota(jnp.int32, (samples, samples), 0)
    order = jnp.where(order, 1.0, 0.0).astype(BF)
    each = samples // LINES
    parts = [q_latent_ref[:, head, :] for head in range(heads)] + [q_rope_ref[...]]
    at = 0
    for part in parts:
        wide = dot(order, part).astype(BF)
        for k, out_ref in enumerate(out_refs):
            out_ref[:, at : at + part.shape[1]] = wide[k * each : (k + 1) * each]
        at += part.shape[1]


def attend_kernel(heads, *refs):
    q_refs, out_refs = refs[:LINES], refs[-LINES:]
    key_refs = refs[LINES : LINES + CORES]
    rope_refs = refs[LINES + CORES : LINES + 2 * CORES]
    w_uv_ref, table_ref = refs[LINES + 2 * CORES : LINES + 2 * CORES + 2]
    lat = key_refs[0].shape[1]
    each = q_refs[0].shape[0] // CORES
    rows = each * LINES
    column = lax.broadcasted_iota(jnp.int32, (rows, VD), 1)
    for core in range(CORES):
        mine = slice(core * each, (core + 1) * each)
        q = jnp.concatenate([ref[mine, :] for ref in q_refs], axis=0)
        keys = key_refs[core][...]
        rope_keys = rope_refs[core][...]
        none = jnp.zeros_like(rope_keys)
        extra = jnp.concatenate([table_ref[mine, :]] * LINES, axis=0).astype(F32)
        for head in range(heads):
            pair = [rope_keys if head == one else none for one in range(heads)]
            score = dot_t(q[:, head * lat : (head + 1) * lat], keys)
            score = (score + dot(q[:, heads * lat :], jnp.concatenate(pair, axis=0))) * SCALE
            best = jnp.max(score, axis=-1, keepdims=True)
            weight = jnp.exp(score - best)
            total = jnp.sum(weight, axis=-1, keepdims=True)
            latent = (dot(weight.astype(BF), keys) / total).astype(BF)
            value = dot(latent, w_uv_ref[head]).astype(BF)
            for k, out_ref in enumerate(out_refs):
                out_ref[mine, head * VD : (head + 1) * VD] = value[k * each : (k + 1) * each]
            for place, piece in enumerate(split_in_kernel(best + jnp.log(total))):
                extra = jnp.where(column == 3 * head + place, piece.astype(F32), extra)
        extra = extra.astype(BF)
        for k, out_ref in enumerate(out_refs):
            out_ref[mine, heads * VD :] = extra[k * each : (k + 1) * each]


def merge_kernel(heads, *refs):
    back_refs = refs[:LINES]
    place_ref, order_ref, self_score_ref, self_latent_ref, w_uv_ref, w_out_ref = refs[LINES:-SIDE]
    out_refs = refs[-SIDE:]
    back = jnp.concatenate([ref[...] for ref in back_refs], axis=0)
    samples = back.shape[0]
    to_place = place_ref[...] == lax.broadcasted_iota(jnp.int32, (samples, samples), 0)
    back = dot_rows(jnp.where(to_place, 1.0, 0.0).astype(BF), back)
    values = []
    for head in range(heads):
        at = heads * VD + 3 * head
        lse = back[:, at : at + 1] + back[:, at + 1 : at + 2] + back[:, at + 2 : at + 3]
        self_score = self_score_ref[:, head : head + 1]
        best = jnp.maximum(lse, self_score)
        cache_part = jnp.exp(lse - best)
        self_part = jnp.exp(self_score - best)
        own_value = dot(self_latent_ref[...], w_uv_ref[head])
        mixed = cache_part * back[:, head * VD : (head + 1) * VD] + self_part * own_value
        values.append((mixed / (cache_part + self_part)).astype(BF))
    rows = dot(order_ref[...], jnp.concatenate(values, axis=1)).astype(BF)
    width = w_out_ref.shape[1] // LINES
    for part in range(LINES):
        columns = slice(part * width, (part + 1) * width)
        total = dot(rows, w_out_ref[:, columns]).astype(BF)
        for k, out_ref in enumerate(out_refs):
            each = out_ref.shape[0]
            out_ref[:, columns] = total[k * each : (k + 1) * each]


def own_rows(half, rows):
    return jnp.where(half == 0, rows[:ROWS], rows[ROWS:])


def with_own(half, rows, residual):
    first = jnp.where(half == 0, residual, 0.0)
    return rows + jnp.concatenate([first, residual - first], axis=0)


def near_kernel(half_ref, *refs):
    part_refs, residual_ref, near_ref, out_ref = refs[:SIDE], refs[SIDE], refs[-2], refs[-1]
    near = sum_wide([ref[...] for ref in part_refs])
    near_ref[...] = near
    out_ref[...] = with_own(half_ref[0], near, residual_ref[...].astype(F32)).astype(BF)


def norm_kernel(half_ref, line_ref, core_ref, near_ref, far_ref, residual_ref, gain_ref, *refs):
    attn_ref, out_refs, scratch = refs[0], refs[1:-1], refs[-1]
    half, line, core = half_ref[0], line_ref[0], core_ref[0]
    total = near_ref[...] + far_ref[...].astype(F32)
    attn_ref[...] = own_rows(half, total).astype(BF)
    mixed = with_own(half, total, residual_ref[...].astype(F32))
    scale = lax.rsqrt(jnp.mean(mixed * mixed, axis=-1, keepdims=True) + NORM_EPS)
    scratch[...] = (mixed * scale * gain_ref[...]).astype(BF)
    share = scratch.shape[1] // GROUPS
    for k, out_ref in enumerate(out_refs):
        chip = lax.rem(line + LINES - k, LINES) * CORES
        for side in range(CORES):
            at = pl.multiple_of((chip + (core + side) % CORES) * share, share)
            out_ref[:, side * share : (side + 1) * share] = scratch[:, pl.ds(at, share)]


def up_kernel(line_ref, rows_ref, *refs):
    w_refs, out_refs, scratches = refs[: 2 * CORES], refs[2 * CORES : -2], refs[-2:]
    each = rows_ref.shape[0] // LINES
    share = rows_ref.shape[1] // CORES
    step = pl.program_id(0)

    @pl.when(step == 0)
    def _():
        line = line_ref[0]
        for place, k in enumerate(FLIP_ORDER):
            for scratch, at in zip(scratches, (lax.rem(line + place, LINES), lax.bitwise_xor(line, k))):
                at = pl.multiple_of(at * each, each)
                scratch[place * each : (place + 1) * each, :] = rows_ref[pl.ds(at, each), :]

    for half, scratch in enumerate(scratches):
        rows = scratch[...]
        total = dot(rows[:, :share], w_refs[half][...]) + dot(rows[:, share:], w_refs[2 + half][...])
        total = total.astype(BF)
        width = total.shape[1]
        at = pl.multiple_of(step * width, width)
        row = 0
        for out_ref in out_refs[:LINES] if half == 0 else out_refs[LINES:]:
            out_ref[:, pl.ds(at, width)] = total[row : row + out_ref.shape[0]]
            row += out_ref.shape[0]


def down_kernel(line_ref, *refs):
    hidden_refs, w_refs, out_ref, total_ref = refs[: LINES + 2], refs[LINES + 2 : -2], refs[-2], refs[-1]
    each = hidden_refs[0].shape[0]
    width = w_refs[0].shape[1]
    line = line_ref[0]
    step = pl.program_id(0)

    def product(rows):
        return [dot(rows, ref[...]) for ref in w_refs]

    @pl.when(step == 0)
    def _():
        totals = product(jnp.concatenate([ref[...] for ref in hidden_refs[:LINES]], axis=0))
        for k in range(LINES):
            at = pl.multiple_of(lax.rem(line + LINES - k, LINES) * each, each)
            for core, total in enumerate(totals):
                total_ref[pl.ds(at, each), core * width : (core + 1) * width] = total[k * each : (k + 1) * each]

    @pl.when(step == 1)
    def _():
        totals = product(jnp.concatenate([ref[...] for ref in hidden_refs[LINES:]], axis=0))
        for place, k in enumerate(FLIP_ORDER):
            at = pl.multiple_of(lax.bitwise_xor(line, k) * each, each)
            for core, total in enumerate(totals):
                columns = slice(core * width, (core + 1) * width)
                whole = total_ref[pl.ds(at, each), columns] + total[place * each : (place + 1) * each]
                out_ref[pl.ds(at, each), columns] = whole.astype(BF)


def whole(shape):
    return pl.BlockSpec(shape, lambda step: (0, 0))


def column_block(one, count):
    return pl.BlockSpec((one.shape[0], one.shape[1] // count), lambda step: (0, step))


def row_block(one, count):
    return pl.BlockSpec((one.shape[0] // count, one.shape[1]), lambda step: (step, 0))


def on_chip(kernel, shapes, *args, dtypes=None, **more):
    vmem = pl.BlockSpec(memory_space=pltpu.VMEM)
    smem = pl.BlockSpec(memory_space=pltpu.SMEM)
    more.setdefault("in_specs", [smem if one.shape == (1,) else vmem for one in args])
    more.setdefault("out_specs", [vmem] * len(shapes))
    return pl.pallas_call(
        kernel,
        out_shape=[
            jax.ShapeDtypeStruct(shape, dtype)
            for shape, dtype in zip(shapes, dtypes or [BF] * len(shapes))
        ],
        compiler_params=pltpu.CompilerParams(vmem_limit_bytes=48 * 1024 * 1024),
        **more,
    )(*args)


def routing_tables(ids, gates, my_half, order):
    tokens = ids.shape[0]
    slots = tokens // ROWS * CAP
    wanted = jnp.arange(PLANES, dtype=jnp.int32) * HALVES + my_half
    hit = ids[:, :, None] == wanted[None, None, :]
    member = jnp.any(hit, axis=1)
    gate_of = jnp.sum(jnp.where(hit, gates[:, :, None], 0.0), axis=1)
    before = jnp.cumsum(member.astype(jnp.int32), axis=0) - member.astype(jnp.int32)
    place = jnp.where(member, before, -1).T
    routed = place[:, None, :] == jnp.arange(slots, dtype=jnp.int32)[None, :, None]
    routed = routed.reshape(PLANES * slots, tokens)
    weights = jnp.where(routed, jnp.repeat(gate_of.T, slots, axis=0), 0.0)
    routing = jnp.take(routed.astype(BF).reshape(PLANES * slots, LINES, -1), order, axis=1)
    return (routing.reshape(PLANES * slots, tokens), *split(weights, 2))


def body(
    q_latent,
    q_rope,
    self_latent,
    self_rope,
    cache_latent,
    cache_rope,
    prompt_of_sample,
    w_uv,
    w_out,
    residual,
    norm_gain,
    expert_ids,
    gate_weight,
    w_gate,
    w_up,
    w_down,
):
    my_half = lax.axis_index("zhi")
    my_core = lax.axis_index("core")
    my_line = lax.axis_index("zlo")
    line = my_line.astype(jnp.int32).reshape(1)
    lines = jnp.arange(LINES, dtype=jnp.int32)
    samples, heads, lat = q_latent.shape
    width = residual.shape[1]
    share = width // GROUPS
    top = expert_ids.shape[1]
    tokens = LINES * HALVES * ROWS
    each = samples // LINES

    def sibling(value):
        return lax.ppermute(value, "core", flips(CORES, 1))

    place = sorted_place(prompt_of_sample, my_line, my_core)[None, :]
    q_sorted = on_chip(
        sort_kernel, [(each, heads * lat + heads * ROPE)] * LINES, q_latent, q_rope, place
    )
    q_here = along_line(q_sorted)
    keys = [cache_latent[0], sibling(cache_latent[0])]
    rope_keys = [cache_rope[0], sibling(cache_rope[0])]

    table = jnp.concatenate([expert_ids.astype(BF), *split(gate_weight, 3)], axis=1)
    stats = 3 * heads
    table_pad = jnp.pad(
        table, ((0, each - table.shape[0]), (stats, VD - stats - table.shape[1]))
    )
    back = on_chip(
        functools.partial(attend_kernel, heads),
        [(each, (heads + 1) * VD)] * LINES,
        *q_here,
        *keys,
        *rope_keys,
        w_uv,
        table_pad,
    )
    back = along_line(back, -1)
    self_wide = self_latent.astype(F32)
    self_pos = self_rope.astype(F32)
    self_score = [
        jnp.sum(q_latent[:, head].astype(F32) * self_wide, axis=-1)
        + jnp.sum(q_rope[:, head * ROPE : (head + 1) * ROPE].astype(F32) * self_pos, axis=-1)
        for head in range(heads)
    ]
    self_score = jnp.stack(self_score, axis=1) * SCALE
    first = on_chip(
        functools.partial(merge_kernel, heads),
        [(samples // SIDE, width)] * SIDE,
        *back,
        place,
        plane_order(my_core),
        self_score,
        self_latent,
        w_uv,
        w_out,
    )
    first = sum_wide([first[0]] + [lax.ppermute(first[k], ALL, plane_shift(k, 0)) for k in (2, 1, 3)])
    first = first.astype(BF).reshape(SIDE, HALVES * ROWS, width)
    second = [first[0]] + [lax.ppermute(first[k], ALL, plane_shift(k, 1)) for k in (1, 2, 3)]
    half = my_half.astype(jnp.int32).reshape(1)
    near, outgoing = on_chip(
        near_kernel,
        [(HALVES * ROWS, width)] * 2,
        half,
        *second,
        residual,
        dtypes=[F32, BF],
    )
    far = lax.ppermute(outgoing, "zhi", flips(HALVES, 1))
    attn_proj, *by_chip = on_chip(
        norm_kernel,
        [(ROWS, width)] + [(HALVES * ROWS, CORES * share)] * LINES,
        half,
        line,
        my_core.astype(jnp.int32).reshape(1),
        near,
        far,
        residual,
        norm_gain.reshape(1, -1),
        scratch_shapes=[pltpu.VMEM((HALVES * ROWS, width), BF)],
    )

    token_rows = jnp.concatenate(along_line(by_chip, -1), axis=0)

    table = jnp.stack([one[:ROWS, heads * VD + stats : heads * VD + stats + 4 * top] for one in back])
    other = lax.ppermute(table, "zhi", flips(HALVES, 1))
    pair = [jnp.where(my_half == 0, table, other), jnp.where(my_half == 0, other, table)]
    table = jnp.concatenate(pair, axis=1)
    table = jnp.take(table, (lines + LINES - my_line) % LINES, axis=0)
    table = table.reshape(tokens, -1).astype(F32)
    gates = table[:, top : 2 * top] + table[:, 2 * top : 3 * top] + table[:, 3 * top : 4 * top]
    routing, gate_hi, gate_lo = routing_tables(
        table[:, :top].astype(jnp.int32), gates, my_half, (lines + my_line) % LINES
    )
    rows_in = exchange(dot(routing, token_rows).astype(BF), XY)

    line_rows = rows_in.shape[0] // LINES
    ups = [w_gate[0], w_up[0], sibling(w_gate[0]), sibling(w_up[0])]
    scalar = pl.BlockSpec(memory_space=pltpu.SMEM)
    ffe = w_gate.shape[2]
    out_shapes = [(line_rows, ffe)] * LINES + [(2 * line_rows, ffe)] * 2
    *gate_parts, up_kept, up_sent = on_chip(
        up_kernel,
        out_shapes,
        line,
        rows_in,
        *ups,
        grid=(UP_STEPS,),
        in_specs=[scalar, whole(rows_in.shape)] + [column_block(one, UP_STEPS) for one in ups],
        out_specs=[whole(shape) for shape in out_shapes],
        scratch_shapes=[pltpu.VMEM(rows_in.shape, BF)] * 2,
    )
    up_sums = sum_wide([up_kept, lax.ppermute(up_sent, "zlo", flips(LINES, 1))])
    gate = sum_wide(along_line(gate_parts))
    up_far = lax.ppermute(up_sums[line_rows:].astype(BF), "zlo", flips(LINES, 2))
    up = up_sums[:line_rows] + up_far.astype(F32)
    hidden = (jax.nn.silu(gate) * up).astype(BF)
    direct, relayed = hidden[:, : ffe // 2], hidden[:, ffe // 2 :]
    relayed = jnp.concatenate([relayed, lax.ppermute(relayed, "zlo", flips(LINES, 2))], axis=0)
    gathered = along_line([direct] * LINES)
    gathered += [relayed, lax.ppermute(relayed, "zlo", flips(LINES, 1))]
    downs = [w_down[0], sibling(w_down[0])]
    out_shape = (rows_in.shape[0], CORES * share)
    (expert_out,) = on_chip(
        down_kernel,
        [out_shape],
        line,
        *gathered,
        *downs,
        grid=(2,),
        in_specs=[scalar] + [whole(one.shape) for one in gathered] + [row_block(one, 2) for one in downs],
        out_specs=[whole(out_shape)],
        scratch_shapes=[pltpu.VMEM(out_shape, F32)],
    )

    returned = exchange(expert_out, XY)
    moe = dot_rows(gate_hi, returned) + dot_rows(gate_lo, returned)
    moe = exchange(moe.astype(BF), ("zlo", "zhi"))
    moe = jnp.sum(moe.reshape(LINES, HALVES, ROWS, CORES, share).astype(F32), axis=1).astype(BF)
    moe = jnp.where(my_core == 0, moe, moe[:, :, ::-1])
    moe_out = moe.transpose(1, 0, 2, 3).reshape(ROWS, width)
    return (attn_proj, moe_out)


def solution(mesh):
    fine = Mesh(mesh.devices.reshape(SIZES), ALL)
    g = GROUP
    e = XY + ("zhi",)
    in_specs = (
        P(g, e, None),
        P(g, e),
        P(g, None),
        P(g, None),
        P(g, None, None),
        P(g, None, None),
        P(g),
        P(e, None, None),
        P(e, None),
        P(g + e, None),
        P(),
        P(g + e, None),
        P(g + e, None),
        P(e, g, None),
        P(e, g, None),
        P(e, None, g),
    )
    out_specs = (P(g + e, None), P(g + e, None))
    return jax.shard_map(body, mesh=fine, in_specs=in_specs, out_specs=out_specs, check_vma=False)
```

```python
import functools

import jax
import jax.numpy as jnp
from jax import lax
from jax.experimental import pallas as pl
from jax.experimental.pallas import tpu as pltpu
from jax.sharding import Mesh, PartitionSpec as P

ROPE = 64
VD = 128
NORM_EPS = 1e-06
SCALE = (VD + ROPE) ** (-0.5)
RUNS = 4
CAP = 3
ROWS = 8
LINE_ORDER = (2, 1, 3)
UP_STEPS = 2
FLIP_ORDER = (0, 2, 1, 3)

SIDE = 4
LINES = 4
CORES = 2
HALVES = 2
GROUPS = LINES * CORES
PLANES = SIDE * SIDE
GROUP = ("zlo", "core")
XY = ("x", "y")
ALL = ("zlo", "core", "x", "y", "zhi")
SIZES = (LINES, CORES, SIDE, SIDE, HALVES)
BF = jnp.bfloat16
F32 = jnp.float32


def dot(a, b):
    return jnp.dot(a, b, preferred_element_type=F32)


def dot_t(a, b):
    return lax.dot_general(a, b, (((1,), (1,)), ((), ())), preferred_element_type=F32)


def dot_rows(a, b):
    return lax.dot_general(a, b, (((0,), (0,)), ((), ())), preferred_element_type=F32)


def split(value, count):
    pieces = []
    for _ in range(count):
        piece = lax.reduce_precision(value, 8, 7)
        pieces.append(piece.astype(BF))
        value = value - piece
    return pieces


def split_in_kernel(value):
    one = value.astype(BF)
    rest = value - one.astype(F32)
    two = rest.astype(BF)
    return one, two, (rest - two.astype(F32)).astype(BF)


def exchange(value, axes):
    return lax.all_to_all(value, axes, 0, 0, tiled=True)


def flips(count, k):
    return [(i, i ^ k) for i in range(count)]


def sum_wide(parts):
    total = parts[0].astype(F32)
    for part in parts[1:]:
        total = total + part.astype(F32)
    return total


def shift(k):
    return [(i, (i + k) % LINES) for i in range(LINES)]


def along_line(parts, sign=1):
    got = {k: lax.ppermute(parts[k], "zlo", shift(sign * k)) for k in LINE_ORDER}
    return [parts[0]] + [got[k] for k in range(1, LINES)]


def plane_shift(k, stage):
    pairs = []

    def number(place):
        flat = 0
        for size, one in zip(SIZES, place):
            flat = flat * size + one
        return flat

    for flat in range(LINES * CORES * PLANES * HALVES):
        place, rest = [], flat
        for size in reversed(SIZES):
            place.insert(0, rest % size)
            rest //= size
        there = list(place)
        axis = 2 if place[1] == stage else 3
        there[axis] = (there[axis] + k) % SIDE
        pairs.append((number(place), number(there)))
    return pairs


def one_hot(source, count):
    return (source[:, None] == jnp.arange(count, dtype=jnp.int32)[None, :]).astype(BF)


def plane_order(my_core):
    me = (lax.axis_index("x"), lax.axis_index("y"))
    row = jnp.arange(PLANES * HALVES * ROWS, dtype=jnp.int32)
    rest = row % (HALVES * ROWS)
    first = row // (HALVES * ROWS) // SIDE
    second = row // (HALVES * ROWS) % SIDE
    x = (me[0] + jnp.where(my_core == 0, first, second)) % SIDE
    y = (me[1] + jnp.where(my_core == 0, second, first)) % SIDE
    return one_hot((x * SIDE + y) * (HALVES * ROWS) + rest, row.shape[0])


def sorted_place(prompt_of_sample, my_line, my_core):
    samples = prompt_of_sample.shape[0]
    block = samples // (GROUPS * RUNS)
    own = prompt_of_sample.reshape(-1, block)[:, 0]
    at = jnp.arange(own.shape[0], dtype=jnp.int32)
    same = (own[:, None] == own[None, :]) & (at[None, :] < at[:, None])
    line = (own // CORES + LINES - my_line) % LINES
    seen = line * CORES + (own % CORES ^ my_core)
    rank = seen * RUNS + jnp.sum(same.astype(jnp.int32), axis=1)
    return jnp.repeat(rank, block) * block + jnp.arange(samples, dtype=jnp.int32) % block


def sort_kernel(q_latent_ref, q_rope_ref, place_ref, *out_refs):
    samples, heads, lat = q_latent_ref.shape
    order = place_ref[...] == lax.broadcasted_iota(jnp.int32, (samples, samples), 0)
    order = jnp.where(order, 1.0, 0.0).astype(BF)
    each = samples // LINES
    parts = [q_latent_ref[:, head, :] for head in range(heads)] + [q_rope_ref[...]]
    at = 0
    for part in parts:
        wide = dot(order, part).astype(BF)
        for k, out_ref in enumerate(out_refs):
            out_ref[:, at : at + part.shape[1]] = wide[k * each : (k + 1) * each]
        at += part.shape[1]


def attend_kernel(heads, *refs):
    q_refs, out_refs = refs[:LINES], refs[-LINES:]
    key_refs = refs[LINES : LINES + CORES]
    rope_refs = refs[LINES + CORES : LINES + 2 * CORES]
    w_uv_ref, table_ref = refs[LINES + 2 * CORES : LINES + 2 * CORES + 2]
    lat = key_refs[0].shape[1]
    each = q_refs[0].shape[0] // CORES
    rows = each * LINES
    column = lax.broadcasted_iota(jnp.int32, (rows, VD), 1)
    for core in range(CORES):
        mine = slice(core * each, (core + 1) * each)
        q = jnp.concatenate([ref[mine, :] for ref in q_refs], axis=0)
        keys = key_refs[core][...]
        rope_keys = rope_refs[core][...]
        none = jnp.zeros_like(rope_keys)
        extra = jnp.concatenate([table_ref[mine, :]] * LINES, axis=0).astype(F32)
        for head in range(heads):
            pair = [rope_keys if head == one else none for one in range(heads)]
            score = dot_t(q[:, head * lat : (head + 1) * lat], keys)
            score = (score + dot(q[:, heads * lat :], jnp.concatenate(pair, axis=0))) * SCALE
            best = jnp.max(score, axis=-1, keepdims=True)
            weight = jnp.exp(score - best)
            total = jnp.sum(weight, axis=-1, keepdims=True)
            latent = (dot(weight.astype(BF), keys) / total).astype(BF)
            value = dot(latent, w_uv_ref[head]).astype(BF)
            for k, out_ref in enumerate(out_refs):
                out_ref[mine, head * VD : (head + 1) * VD] = value[k * each : (k + 1) * each]
            for place, piece in enumerate(split_in_kernel(best + jnp.log(total))):
                extra = jnp.where(column == 3 * head + place, piece.astype(F32), extra)
        extra = extra.astype(BF)
        for k, out_ref in enumerate(out_refs):
            out_ref[mine, heads * VD :] = extra[k * each : (k + 1) * each]


def merge_kernel(heads, *refs):
    back_refs = refs[:LINES]
    place_ref, order_ref, self_score_ref, self_latent_ref, w_uv_ref, w_out_ref = refs[LINES:-SIDE]
    out_refs = refs[-SIDE:]
    back = jnp.concatenate([ref[...] for ref in back_refs], axis=0)
    samples = back.shape[0]
    to_place = place_ref[...] == lax.broadcasted_iota(jnp.int32, (samples, samples), 0)
    back = dot_rows(jnp.where(to_place, 1.0, 0.0).astype(BF), back)
    values = []
    for head in range(heads):
        at = heads * VD + 3 * head
        lse = back[:, at : at + 1] + back[:, at + 1 : at + 2] + back[:, at + 2 : at + 3]
        self_score = self_score_ref[:, head : head + 1]
        best = jnp.maximum(lse, self_score)
        cache_part = jnp.exp(lse - best)
        self_part = jnp.exp(self_score - best)
        own_value = dot(self_latent_ref[...], w_uv_ref[head])
        mixed = cache_part * back[:, head * VD : (head + 1) * VD] + self_part * own_value
        values.append((mixed / (cache_part + self_part)).astype(BF))
    rows = dot(order_ref[...], jnp.concatenate(values, axis=1)).astype(BF)
    width = w_out_ref.shape[1] // LINES
    for part in range(LINES):
        columns = slice(part * width, (part + 1) * width)
        total = dot(rows, w_out_ref[:, columns]).astype(BF)
        for k, out_ref in enumerate(out_refs):
            each = out_ref.shape[0]
            out_ref[:, columns] = total[k * each : (k + 1) * each]


def own_rows(half, rows):
    return jnp.where(half == 0, rows[:ROWS], rows[ROWS:])


def with_own(half, rows, residual):
    first = jnp.where(half == 0, residual, 0.0)
    return rows + jnp.concatenate([first, residual - first], axis=0)


def near_kernel(half_ref, *refs):
    part_refs, residual_ref, near_ref, out_ref = refs[:SIDE], refs[SIDE], refs[-2], refs[-1]
    near = sum_wide([ref[...] for ref in part_refs])
    near_ref[...] = near
    out_ref[...] = with_own(half_ref[0], near, residual_ref[...].astype(F32)).astype(BF)


def norm_kernel(half_ref, line_ref, core_ref, near_ref, far_ref, residual_ref, gain_ref, *refs):
    attn_ref, out_refs, scratch = refs[0], refs[1:-1], refs[-1]
    half, line, core = half_ref[0], line_ref[0], core_ref[0]
    total = near_ref[...] + far_ref[...].astype(F32)
    attn_ref[...] = own_rows(half, total).astype(BF)
    mixed = with_own(half, total, residual_ref[...].astype(F32))
    scale = lax.rsqrt(jnp.mean(mixed * mixed, axis=-1, keepdims=True) + NORM_EPS)
    scratch[...] = (mixed * scale * gain_ref[...]).astype(BF)
    share = scratch.shape[1] // GROUPS
    for k, out_ref in enumerate(out_refs):
        chip = lax.rem(line + LINES - k, LINES) * CORES
        for side in range(CORES):
            at = pl.multiple_of((chip + (core + side) % CORES) * share, share)
            out_ref[:, side * share : (side + 1) * share] = scratch[:, pl.ds(at, share)]


def up_kernel(line_ref, rows_ref, *refs):
    w_refs, out_refs, scratches = refs[: 2 * CORES], refs[2 * CORES : -2], refs[-2:]
    each = rows_ref.shape[0] // LINES
    share = rows_ref.shape[1] // CORES
    step = pl.program_id(0)

    @pl.when(step == 0)
    def _():
        line = line_ref[0]
        for place, k in enumerate(FLIP_ORDER):
            for scratch, at in zip(scratches, (lax.rem(line + place, LINES), lax.bitwise_xor(line, k))):
                at = pl.multiple_of(at * each, each)
                scratch[place * each : (place + 1) * each, :] = rows_ref[pl.ds(at, each), :]

    for half, scratch in enumerate(scratches):
        rows = scratch[...]
        total = dot(rows[:, :share], w_refs[half][...]) + dot(rows[:, share:], w_refs[2 + half][...])
        total = total.astype(BF)
        width = total.shape[1]
        at = pl.multiple_of(step * width, width)
        row = 0
        for out_ref in out_refs[:LINES] if half == 0 else out_refs[LINES:]:
            out_ref[:, pl.ds(at, width)] = total[row : row + out_ref.shape[0]]
            row += out_ref.shape[0]


def down_kernel(line_ref, *refs):
    hidden_refs, w_refs, out_ref, total_ref = refs[: LINES + 2], refs[LINES + 2 : -2], refs[-2], refs[-1]
    each = hidden_refs[0].shape[0]
    width = w_refs[0].shape[1]
    line = line_ref[0]
    step = pl.program_id(0)

    def product(rows):
        return [dot(rows, ref[...]) for ref in w_refs]

    @pl.when(step == 0)
    def _():
        totals = product(jnp.concatenate([ref[...] for ref in hidden_refs[:LINES]], axis=0))
        for k in range(LINES):
            at = pl.multiple_of(lax.rem(line + LINES - k, LINES) * each, each)
            for core, total in enumerate(totals):
                total_ref[pl.ds(at, each), core * width : (core + 1) * width] = total[k * each : (k + 1) * each]

    @pl.when(step == 1)
    def _():
        totals = product(jnp.concatenate([ref[...] for ref in hidden_refs[LINES:]], axis=0))
        for place, k in enumerate(FLIP_ORDER):
            at = pl.multiple_of(lax.bitwise_xor(line, k) * each, each)
            for core, total in enumerate(totals):
                columns = slice(core * width, (core + 1) * width)
                whole = total_ref[pl.ds(at, each), columns] + total[place * each : (place + 1) * each]
                out_ref[pl.ds(at, each), columns] = whole.astype(BF)


def whole(shape):
    return pl.BlockSpec(shape, lambda step: (0, 0))


def column_block(one, count):
    return pl.BlockSpec((one.shape[0], one.shape[1] // count), lambda step: (0, step))


def row_block(one, count):
    return pl.BlockSpec((one.shape[0] // count, one.shape[1]), lambda step: (step, 0))


def on_chip(kernel, shapes, *args, dtypes=None, **more):
    vmem = pl.BlockSpec(memory_space=pltpu.VMEM)
    smem = pl.BlockSpec(memory_space=pltpu.SMEM)
    more.setdefault("in_specs", [smem if one.shape == (1,) else vmem for one in args])
    more.setdefault("out_specs", [vmem] * len(shapes))
    return pl.pallas_call(
        kernel,
        out_shape=[
            jax.ShapeDtypeStruct(shape, dtype)
            for shape, dtype in zip(shapes, dtypes or [BF] * len(shapes))
        ],
        compiler_params=pltpu.CompilerParams(vmem_limit_bytes=48 * 1024 * 1024),
        **more,
    )(*args)


def routing_tables(ids, gates, my_half, order):
    tokens = ids.shape[0]
    slots = tokens // ROWS * CAP
    wanted = jnp.arange(PLANES, dtype=jnp.int32) * HALVES + my_half
    hit = ids[:, :, None] == wanted[None, None, :]
    member = jnp.any(hit, axis=1)
    gate_of = jnp.sum(jnp.where(hit, gates[:, :, None], 0.0), axis=1)
    before = jnp.cumsum(member.astype(jnp.int32), axis=0) - member.astype(jnp.int32)
    place = jnp.where(member, before, -1).T
    routed = place[:, None, :] == jnp.arange(slots, dtype=jnp.int32)[None, :, None]
    routed = routed.reshape(PLANES * slots, tokens)
    weights = jnp.where(routed, jnp.repeat(gate_of.T, slots, axis=0), 0.0)
    routing = jnp.take(routed.astype(BF).reshape(PLANES * slots, LINES, -1), order, axis=1)
    return (routing.reshape(PLANES * slots, tokens), *split(weights, 2))


def body(
    q_latent,
    q_rope,
    self_latent,
    self_rope,
    cache_latent,
    cache_rope,
    prompt_of_sample,
    w_uv,
    w_out,
    residual,
    norm_gain,
    expert_ids,
    gate_weight,
    w_gate,
    w_up,
    w_down,
):
    my_half = lax.axis_index("zhi")
    my_core = lax.axis_index("core")
    my_line = lax.axis_index("zlo")
    line = my_line.astype(jnp.int32).reshape(1)
    lines = jnp.arange(LINES, dtype=jnp.int32)
    samples, heads, lat = q_latent.shape
    width = residual.shape[1]
    share = width // GROUPS
    top = expert_ids.shape[1]
    tokens = LINES * HALVES * ROWS
    each = samples // LINES

    def sibling(value):
        return lax.ppermute(value, "core", flips(CORES, 1))

    place = sorted_place(prompt_of_sample, my_line, my_core)[None, :]
    q_sorted = on_chip(
        sort_kernel, [(each, heads * lat + heads * ROPE)] * LINES, q_latent, q_rope, place
    )
    q_here = along_line(q_sorted)
    keys = [cache_latent[0], sibling(cache_latent[0])]
    rope_keys = [cache_rope[0], sibling(cache_rope[0])]

    table = jnp.concatenate([expert_ids.astype(BF), *split(gate_weight, 3)], axis=1)
    stats = 3 * heads
    table_pad = jnp.pad(
        table, ((0, each - table.shape[0]), (stats, VD - stats - table.shape[1]))
    )
    back = on_chip(
        functools.partial(attend_kernel, heads),
        [(each, (heads + 1) * VD)] * LINES,
        *q_here,
        *keys,
        *rope_keys,
        w_uv,
        table_pad,
    )
    back = along_line(back, -1)
    self_wide = self_latent.astype(F32)
    self_pos = self_rope.astype(F32)
    self_score = [
        jnp.sum(q_latent[:, head].astype(F32) * self_wide, axis=-1)
        + jnp.sum(q_rope[:, head * ROPE : (head + 1) * ROPE].astype(F32) * self_pos, axis=-1)
        for head in range(heads)
    ]
    self_score = jnp.stack(self_score, axis=1) * SCALE
    first = on_chip(
        functools.partial(merge_kernel, heads),
        [(samples // SIDE, width)] * SIDE,
        *back,
        place,
        plane_order(my_core),
        self_score,
        self_latent,
        w_uv,
        w_out,
    )
    first = sum_wide([first[0]] + [lax.ppermute(first[k], ALL, plane_shift(k, 0)) for k in (2, 1, 3)])
    first = first.astype(BF).reshape(SIDE, HALVES * ROWS, width)
    second = [first[0]] + [lax.ppermute(first[k], ALL, plane_shift(k, 1)) for k in (1, 2, 3)]
    half = my_half.astype(jnp.int32).reshape(1)
    near, outgoing = on_chip(
        near_kernel,
        [(HALVES * ROWS, width)] * 2,
        half,
        *second,
        residual,
        dtypes=[F32, BF],
    )
    far = lax.ppermute(outgoing, "zhi", flips(HALVES, 1))
    attn_proj, *by_chip = on_chip(
        norm_kernel,
        [(ROWS, width)] + [(HALVES * ROWS, CORES * share)] * LINES,
        half,
        line,
        my_core.astype(jnp.int32).reshape(1),
        near,
        far,
        residual,
        norm_gain.reshape(1, -1),
        scratch_shapes=[pltpu.VMEM((HALVES * ROWS, width), BF)],
    )

    token_rows = jnp.concatenate(along_line(by_chip, -1), axis=0)

    table = jnp.stack([one[:ROWS, heads * VD + stats : heads * VD + stats + 4 * top] for one in back])
    other = lax.ppermute(table, "zhi", flips(HALVES, 1))
    pair = [jnp.where(my_half == 0, table, other), jnp.where(my_half == 0, other, table)]
    table = jnp.concatenate(pair, axis=1)
    table = jnp.take(table, (lines + LINES - my_line) % LINES, axis=0)
    table = table.reshape(tokens, -1).astype(F32)
    gates = table[:, top : 2 * top] + table[:, 2 * top : 3 * top] + table[:, 3 * top : 4 * top]
    routing, gate_hi, gate_lo = routing_tables(
        table[:, :top].astype(jnp.int32), gates, my_half, (lines + my_line) % LINES
    )
    rows_in = exchange(dot(routing, token_rows).astype(BF), XY)

    line_rows = rows_in.shape[0] // LINES
    ups = [w_gate[0], w_up[0], sibling(w_gate[0]), sibling(w_up[0])]
    scalar = pl.BlockSpec(memory_space=pltpu.SMEM)
    ffe = w_gate.shape[2]
    out_shapes = [(line_rows, ffe)] * LINES + [(2 * line_rows, ffe)] * 2
    *gate_parts, up_kept, up_sent = on_chip(
        up_kernel,
        out_shapes,
        line,
        rows_in,
        *ups,
        grid=(UP_STEPS,),
        in_specs=[scalar, whole(rows_in.shape)] + [column_block(one, UP_STEPS) for one in ups],
        out_specs=[whole(shape) for shape in out_shapes],
        scratch_shapes=[pltpu.VMEM(rows_in.shape, BF)] * 2,
    )
    up_sums = sum_wide([up_kept, lax.ppermute(up_sent, "zlo", flips(LINES, 1))])
    gate = sum_wide(along_line(gate_parts))
    up_far = lax.ppermute(up_sums[line_rows:].astype(BF), "zlo", flips(LINES, 2))
    up = up_sums[:line_rows] + up_far.astype(F32)
    hidden = (jax.nn.silu(gate) * up).astype(BF)
    direct, relayed = hidden[:, : ffe // 2], hidden[:, ffe // 2 :]
    relayed = jnp.concatenate([relayed, lax.ppermute(relayed, "zlo", flips(LINES, 2))], axis=0)
    gathered = along_line([direct] * LINES)
    gathered += [relayed, lax.ppermute(relayed, "zlo", flips(LINES, 1))]
    downs = [w_down[0], sibling(w_down[0])]
    out_shape = (rows_in.shape[0], CORES * share)
    (expert_out,) = on_chip(
        down_kernel,
        [out_shape],
        line,
        *gathered,
        *downs,
        grid=(2,),
        in_specs=[scalar] + [whole(one.shape) for one in gathered] + [row_block(one, 2) for one in downs],
        out_specs=[whole(out_shape)],
        scratch_shapes=[pltpu.VMEM(out_shape, F32)],
    )

    returned = exchange(expert_out, XY)
    moe = dot_rows(gate_hi, returned) + dot_rows(gate_lo, returned)
    moe = exchange(moe.astype(BF), ("zlo", "zhi"))
    moe = jnp.sum(moe.reshape(LINES, HALVES, ROWS, CORES, share).astype(F32), axis=1).astype(BF)
    moe = jnp.where(my_core == 0, moe, moe[:, :, ::-1])
    moe_out = moe.transpose(1, 0, 2, 3).reshape(ROWS, width)
    return (attn_proj, moe_out)


def solution(mesh):
    fine = Mesh(mesh.devices.reshape(SIZES), ALL)
    g = GROUP
    e = XY + ("zhi",)
    in_specs = (
        P(g, e, None),
        P(g, e),
        P(g, None),
        P(g, None),
        P(g, None, None),
        P(g, None, None),
        P(g),
        P(e, None, None),
        P(e, None),
        P(g + e, None),
        P(),
        P(g + e, None),
        P(g + e, None),
        P(e, g, None),
        P(e, g, None),
        P(e, None, g),
    )
    out_specs = (P(g + e, None), P(g + e, None))
    return jax.shard_map(body, mesh=fine, in_specs=in_specs, out_specs=out_specs, check_vma=False)
```
